32 devices in a mesh: groups: 2 (over x), seq: 16 (over z, y, core).
Axes of the slice: x: 2, y: 2, z: 4, core: 2. Of those that a mesh axis runs over, the one named last changes fastest.
Arguments:
- query_rows: bfloat16 [6144, 2048], P(('groups', 'seq')), parts along dimension 0, may hold values from -5.5 to 5.5, as said below
- key_rows: bfloat16 [6144, 2048], P(('groups', 'seq')), parts along dimension 0, may hold values from -5.5 to 5.5, as said below
- value_rows: bfloat16 [6144, 2048], P(('groups', 'seq')), parts along dimension 0, may hold values from -6 to 6
- out_grad: bfloat16 [6144, 2048], P(('groups', 'seq')), parts along dimension 0, may hold values from -6 to 6
Outputs:
- attended: bfloat16 [6144, 2048], P(('groups', 'seq')), parts along dimension 0
- query_grad: bfloat16 [6144, 2048], P(('groups', 'seq')), parts along dimension 0
- key_grad: bfloat16 [6144, 2048], P(('groups', 'seq')), parts along dimension 0
- value_grad: bfloat16 [6144, 2048], P(('groups', 'seq')), parts along dimension 0
The draws below stay inside these ranges and needn't reach their ends.
There are 2 independent parts, one for each index of `groups`. The reference program is written for one: setup_inputs(seed, part) draws one part's arguments, and reference() takes and returns one part's arrays. A program takes and returns all parts, laid end to end along the dimension named above; each array names one. Nothing has to cross between parts.
Inputs may be any that keep to these rules, and one draw needn't show every extreme that they name: `query_rows`: queries of order one. `key_rows`: keys of order one.
All inputs are finite; a program needn't handle non-finite values.
Results may differ from the reference program's by a relative error of at most 0.017.
Values may be sent and summed in bfloat16 or wider, within the bound.
A program may use at most 128 MiB of HBM per device.

```python
import math
import jax
import jax.numpy as jnp
from jax import lax

HEADS = 16
HEAD_DIM = 128
BLOCK = 128
FEAT = 2048
OFF = 32
TOKENS = 3072


def paired_rows(key):
    base_key = jax.random.fold_in(key, 7)
    first_key, second_key = jax.random.split(base_key, 2)
    dims_full = (TOKENS, HEADS * HEAD_DIM)
    queries = jnp.clip(jax.random.normal(first_key, dims_full, jnp.float32), -5.5, 5.5)
    keys_out = jnp.clip(jax.random.normal(second_key, dims_full, jnp.float32), -5.5, 5.5)
    return (queries, keys_out)


def draw_query_rows(key, part):
    return paired_rows(key)[0].astype(jnp.bfloat16)


def draw_key_rows(key, part):
    return paired_rows(key)[1].astype(jnp.bfloat16)


def steps_of(own_key, shape, cuts, least, high):
    factor_of = 1.0
    for dim, blocks in cuts:
        draws = jax.random.uniform(jax.random.fold_in(jax.random.fold_in(own_key, 6), dim), (blocks,), jnp.float32, least / len(cuts), high / len(cuts))
        factor_of = factor_of * jnp.repeat(jnp.exp(draws), shape[dim] // blocks).reshape((-1,) + (1,) * (len(shape) - 1 - dim))
    return factor_of


def gaussian(stream_key, extent, scale, limit, pieces=(), held_as=jnp.bfloat16):
    values = jax.random.normal(stream_key, extent, jnp.float32) * scale
    if len(pieces) > 0:
        values = steps_of(stream_key, extent, pieces, -0.22, 0.18) * values
    return jnp.clip(values, min=-limit, max=limit).astype(held_as)


def setup_inputs(seed: int = 0, part: int = 0) -> dict:
    keys = jax.random.split(jax.random.key(seed), 5)
    own_keys = jax.random.split(jax.random.fold_in(keys[4], part), 5)
    query_rows = draw_query_rows(jax.random.fold_in(jax.random.fold_in(keys[4], part), 71), part)
    key_rows = draw_key_rows(jax.random.fold_in(jax.random.fold_in(keys[4], part), 71), part)
    value_rows = gaussian(own_keys[2], (TOKENS, FEAT), 1.0, 6.0, ((0, 16),))
    out_grad = gaussian(own_keys[3], (TOKENS, FEAT), 1.0, 6.0, ((0, 16),))
    return {"query_rows": query_rows, "key_rows": key_rows, "value_rows": value_rows, "out_grad": out_grad}


def head_pass(operands):
    queries, keys_head, values_head, cotangent = operands
    scale = 1.0 / math.sqrt(HEAD_DIM)
    blocks = TOKENS // BLOCK + 1

    def padded(array):
        return jnp.pad(array.astype(jnp.float32), ((OFF, BLOCK - OFF), (0, 0))).reshape(blocks, BLOCK, HEAD_DIM)
    q_blocks = padded(queries)
    k_blocks = padded(keys_head)
    v_blocks = padded(values_head)
    g_blocks = padded(cotangent)
    k_summary = k_blocks[:, BLOCK - 1, :]
    v_summary = v_blocks[:, BLOCK - 1, :]
    local_scores = jnp.einsum('nid,njd->nij', q_blocks, k_blocks) * scale
    summary_scores = jnp.einsum('nid,md->nim', q_blocks, k_summary) * scale
    live = (jnp.arange(blocks * BLOCK, dtype=jnp.int32) >= OFF).reshape(blocks, BLOCK)
    causal = jnp.tril(jnp.ones((BLOCK, BLOCK), dtype=bool))[None, :, :]
    causal = causal & (live[:, None, :] | jnp.logical_not(live[:, :, None]))
    block_ids = jnp.arange(blocks, dtype=jnp.int32)
    earlier = (block_ids[None, :] < block_ids[:, None])[:, None, :]
    top = jnp.maximum(lax.optimization_barrier(jnp.max(jnp.where(causal, local_scores, -jnp.inf), axis=-1)), lax.optimization_barrier(jnp.max(jnp.where(earlier, summary_scores, -jnp.inf), axis=-1)))
    local_exp = jnp.where(causal, jnp.exp(local_scores - top[..., None]), 0.0)
    summary_exp = jnp.where(earlier, jnp.exp(summary_scores - top[..., None]), 0.0)
    total = lax.optimization_barrier(jnp.sum(local_exp, axis=-1)) + lax.optimization_barrier(jnp.sum(summary_exp, axis=-1))
    local_prob = local_exp / total[..., None]
    summary_prob = summary_exp / total[..., None]
    local_weights = local_prob.astype(jnp.bfloat16).astype(jnp.float32)
    summary_weights = summary_prob.astype(jnp.bfloat16).astype(jnp.float32)
    out_full = jnp.einsum('nij,njd->nid', local_weights, v_blocks) + jnp.einsum('nim,md->nid', summary_weights, v_summary)
    attended = out_full.astype(jnp.bfloat16)
    delta = lax.optimization_barrier(jnp.sum(g_blocks * attended.astype(jnp.float32), axis=-1))
    local_dw = jnp.einsum('nid,njd->nij', g_blocks, v_blocks)
    summary_dw = jnp.einsum('nid,md->nim', g_blocks, v_summary)
    local_ds = (local_prob * (local_dw - delta[..., None])).astype(jnp.bfloat16).astype(jnp.float32)
    summary_ds = (summary_prob * (summary_dw - delta[..., None])).astype(jnp.bfloat16).astype(jnp.float32)
    query_grad = scale * (jnp.einsum('nij,njd->nid', local_ds, k_blocks) + jnp.einsum('nim,md->nid', summary_ds, k_summary))
    key_local = jnp.einsum('nij,nid->njd', local_ds, q_blocks)
    key_summary = jnp.einsum('nim,nid->md', summary_ds, q_blocks)
    key_full = key_local.at[:, BLOCK - 1, :].add(key_summary)
    value_local = jnp.einsum('nij,nid->njd', local_weights, g_blocks)
    value_summary = jnp.einsum('nim,nid->md', summary_weights, g_blocks)
    value_full = value_local.at[:, BLOCK - 1, :].add(value_summary)

    def unpad(array):
        return array.reshape(blocks * BLOCK, HEAD_DIM)[OFF:OFF + TOKENS]
    return (unpad(attended), unpad(query_grad.astype(jnp.bfloat16)), unpad((scale * key_full).astype(jnp.bfloat16)), unpad(value_full.astype(jnp.bfloat16)))

def split_heads(array):
    return array.reshape(TOKENS, HEADS, HEAD_DIM).transpose(1, 0, 2)

def merge_heads(array):
    return array.transpose(1, 0, 2).reshape(TOKENS, HEADS * HEAD_DIM)

def reference(query_rows, key_rows, value_rows, out_grad):
    results = lax.map(head_pass, (split_heads(query_rows), split_heads(key_rows), split_heads(value_rows), split_heads(out_grad)))
    return (merge_heads(results[0]), merge_heads(results[1]), merge_heads(results[2]), merge_heads(results[3]))
```

```python
import functools
import math

import jax
import jax.numpy as jnp
from jax import lax
from jax.experimental import pallas as pl
from jax.experimental.pallas import tpu as pltpu
from jax.sharding import PartitionSpec as P

HEADS = 16
HEAD_DIM = 128
BLOCK = 128
OFF = 32
TAIL = 96
SLOT_DEV = 2
HEADS_STEP = 4
SCALE = 1.0 / math.sqrt(HEAD_DIM)
NEG = -1e30


def shifted(block, axis, distance):
    devices = range(lax.axis_size(axis))
    route = [(i - distance, i) for i in devices if i - distance in devices]
    return lax.ppermute(block, axis, route)


def bias_of(shard, rows, slots):
    first = shard * rows
    shape = (rows, TAIL + rows)
    query = first + lax.broadcasted_iota(jnp.int32, shape, 0)
    pos = first - TAIL + lax.broadcasted_iota(jnp.int32, shape, 1)
    local = (pos >= 0) & (pos <= query) & ((pos + OFF) >> 7 == (query + OFF) >> 7)
    shape = (rows, slots)
    query = first + lax.broadcasted_iota(jnp.int32, shape, 0)
    slot = lax.broadcasted_iota(jnp.int32, shape, 1)
    start = (slot >> 1) * rows
    offset = BLOCK - 1 - ((start + OFF) & (BLOCK - 1)) + BLOCK * (slot & 1)
    summary = (offset < rows) & ((start + offset + OFF) >> 7 < (query + OFF) >> 7)
    return (
        jnp.where(local, 0.0, NEG).astype(jnp.float32),
        jnp.where(summary, 0.0, NEG).astype(jnp.float32),
    )


def dot(a, b, dims):
    return lax.dot_general(a, b, (dims, ((), ())), preferred_element_type=jnp.float32)


NT = ((1,), (1,))
NN = ((1,), (0,))
TN = ((0,), (0,))


def one_head(q, k, v, g, bias):
    scores = dot(q, k, NT) * SCALE + bias
    top = jnp.max(scores, axis=1, keepdims=True)
    expo = jnp.exp(scores - top)
    prob = expo * (1.0 / jnp.sum(expo, axis=1, keepdims=True))
    weights = prob.astype(jnp.bfloat16)
    attended = dot(weights, v, NN).astype(jnp.bfloat16)
    delta = jnp.sum(g.astype(jnp.float32) * attended.astype(jnp.float32), axis=1, keepdims=True)
    dscores = (prob * (dot(g, v, NT) - delta)).astype(jnp.bfloat16)
    qgrad = (dot(dscores, k, NN) * SCALE).astype(jnp.bfloat16)
    return attended, qgrad, dot(dscores, q, TN) * SCALE, dot(weights, g, TN)


def kernel(q_ref, k_ref, v_ref, g_ref, halo_ref, slot_ref, out_ref, qg_ref, kg_ref, vg_ref,
           hg_ref, sg_ref, bias_ref):
    rows = q_ref.shape[0]
    slots = slot_ref.shape[1]

    @pl.when(pl.program_id(0) == 0)
    def _():
        local, summary = bias_of(lax.axis_index("seq"), rows, slots)
        bias_ref[:, : TAIL + rows] = local
        bias_ref[:, TAIL + rows :] = summary

    for h in range(HEADS_STEP):
        c = slice(h * HEAD_DIM, (h + 1) * HEAD_DIM)
        k = jnp.concatenate([halo_ref[0, :, c], k_ref[:, c], slot_ref[0, :, c]], axis=0)
        v = jnp.concatenate([halo_ref[1, :, c], v_ref[:, c], slot_ref[1, :, c]], axis=0)
        attended, qgrad, kg, vg = one_head(q_ref[:, c], k, v, g_ref[:, c], bias_ref[...])
        out_ref[:, c] = attended
        qg_ref[:, c] = qgrad
        for i, (grad, own_ref) in enumerate(((kg, kg_ref), (vg, vg_ref))):
            hg_ref[i, :, c] = grad[:TAIL].astype(jnp.bfloat16)
            own_ref[:, c] = grad[TAIL : TAIL + rows]
            sg_ref[i, :, c] = grad[TAIL + rows :].astype(jnp.bfloat16)


def attention(query_rows, key_rows, value_rows, out_grad, halo, slots):
    rows, feats = query_rows.shape
    count = slots.shape[1]
    wide = HEADS_STEP * HEAD_DIM
    own = pl.BlockSpec((rows, wide), lambda i: (0, i))
    tail = pl.BlockSpec((2, TAIL, wide), lambda i: (0, 0, i))
    slot = pl.BlockSpec((2, count, wide), lambda i: (0, 0, i))
    columns = TAIL + rows + count
    return pl.pallas_call(
        kernel,
        grid=(feats // wide,),
        in_specs=[own, own, own, own, tail, slot],
        out_specs=[own, own, own, own, tail, slot],
        out_shape=[
            jax.ShapeDtypeStruct((rows, feats), jnp.bfloat16),
            jax.ShapeDtypeStruct((rows, feats), jnp.bfloat16),
            jax.ShapeDtypeStruct((rows, feats), jnp.float32),
            jax.ShapeDtypeStruct((rows, feats), jnp.float32),
            jax.ShapeDtypeStruct((2, TAIL, feats), jnp.bfloat16),
            jax.ShapeDtypeStruct((2, count, feats), jnp.bfloat16),
        ],
        scratch_shapes=[pltpu.VMEM((rows, columns), jnp.float32)],
        compiler_params=pltpu.CompilerParams(vmem_limit_bytes=40 * 1024 * 1024),
        cost_estimate=pl.CostEstimate(
            flops=10 * rows * columns * feats,
            bytes_accessed=24 * rows * feats,
            transcendentals=HEADS * rows * columns,
        ),
    )(query_rows, key_rows, value_rows, out_grad, halo, slots)


def body(query_rows, key_rows, value_rows, out_grad):
    rows, feats = query_rows.shape
    shard = lax.axis_index("seq")
    shards = lax.axis_size("seq")
    lead = (shard * rows + OFF) % BLOCK
    halo = shifted(jnp.stack([key_rows[rows - TAIL :], value_rows[rows - TAIL :]]), "seq", 1)
    index = [BLOCK - 1 - lead + BLOCK * i for i in range(SLOT_DEV)]
    own_slots = jnp.stack([
        jnp.concatenate([
            jnp.where(i < rows, lax.dynamic_slice_in_dim(array, jnp.minimum(i, rows - 1), 1, 0), 0)
            for i in index
        ])
        for array in (key_rows, value_rows)
    ])
    slots = lax.all_gather(own_slots, "seq", axis=1, tiled=True)
    attended, query_grad, key_own, value_own, halo_grad, slot_grad = attention(
        query_rows, key_rows, value_rows, out_grad, halo, slots
    )
    after = shifted(halo_grad, "seq", -1)
    parts = lax.all_to_all(
        slot_grad.reshape(2, shards, SLOT_DEV, feats), "seq", split_axis=1, concat_axis=1, tiled=True
    )
    mine = jnp.sum(parts.astype(jnp.float32), axis=1)
    row = jnp.arange(rows, dtype=jnp.int32)[:, None]

    def total(own, i):
        grad = own + jnp.pad(after[i].astype(jnp.float32), ((rows - TAIL, 0), (0, 0)))
        for s in range(SLOT_DEV):
            grad = grad + jnp.where(row == index[s], mine[i, s][None, :], 0.0)
        return grad.astype(jnp.bfloat16)

    return attended, query_grad, total(key_own, 0), total(value_own, 1)


def solution(mesh):
    spec = P(("groups", "seq"), None)
    return jax.shard_map(
        body, mesh=mesh, in_specs=(spec,) * 4, out_specs=(spec,) * 4, check_vma=False
    )
```

```python
import functools
import math

import jax
import jax.numpy as jnp
from jax import lax
from jax.experimental import pallas as pl
from jax.experimental.pallas import tpu as pltpu
from jax.sharding import PartitionSpec as P

HEADS = 16
HEAD_DIM = 128
BLOCK = 128
OFF = 32
TAIL = 96
SLOT_DEV = 2
HEADS_STEP = 4
SCALE = 1.0 / math.sqrt(HEAD_DIM)
NEG = -1e30


def bias_of(shard, rows, slots):
    first = shard * rows
    shape = (rows, TAIL + rows)
    query = first + lax.broadcasted_iota(jnp.int32, shape, 0)
    pos = first - TAIL + lax.broadcasted_iota(jnp.int32, shape, 1)
    local = (pos >= 0) & (pos <= query) & ((pos + OFF) >> 7 == (query + OFF) >> 7)
    shape = (rows, slots)
    query = first + lax.broadcasted_iota(jnp.int32, shape, 0)
    slot = lax.broadcasted_iota(jnp.int32, shape, 1)
    start = (slot >> 1) * rows
    offset = BLOCK - 1 - ((start + OFF) & (BLOCK - 1)) + BLOCK * (slot & 1)
    summary = (offset < rows) & ((start + offset + OFF) >> 7 < (query + OFF) >> 7)
    return (
        jnp.where(local, 0.0, NEG).astype(jnp.float32),
        jnp.where(summary, 0.0, NEG).astype(jnp.float32),
    )


def dot(a, b, dims):
    return lax.dot_general(a, b, (dims, ((), ())), preferred_element_type=jnp.float32)


NT = ((1,), (1,))
NN = ((1,), (0,))
TN = ((0,), (0,))


def one_head(q, k, v, g, bias):
    scores = dot(q, k, NT) * SCALE + bias
    top = jnp.max(scores, axis=1, keepdims=True)
    expo = jnp.exp(scores - top)
    prob = expo * (1.0 / jnp.sum(expo, axis=1, keepdims=True))
    weights = prob.astype(jnp.bfloat16)
    attended = dot(weights, v, NN).astype(jnp.bfloat16)
    delta = jnp.sum(g.astype(jnp.float32) * attended.astype(jnp.float32), axis=1, keepdims=True)
    dscores = (prob * (dot(g, v, NT) - delta)).astype(jnp.bfloat16)
    qgrad = (dot(dscores, k, NN) * SCALE).astype(jnp.bfloat16)
    return attended, qgrad, dot(dscores, q, TN) * SCALE, dot(weights, g, TN)


def remote(src, dst, send, recv, seq):
    return pltpu.make_async_remote_copy(
        src_ref=src, dst_ref=dst, send_sem=send, recv_sem=recv,
        device_id={"seq": seq}, device_id_type=pl.DeviceIdType.MESH,
    )


def kernel(shards, q_ref, k_ref, v_ref, g_ref, mine_ref, out_ref, qg_ref, kg_ref, vg_ref, after_ref,
           sum_ref, bias_ref, halo_ref, hg_ref, slot_ref, part_ref, got_ref, ks_ref, vs_ref,
           kp_ref, vp_ref, halo_send, halo_recv, slot_send, slot_recv, back_send, back_recv,
           part_send, part_recv):
    rows, feats = q_ref.shape
    slots = shards * SLOT_DEV
    half = SLOT_DEV * HEADS
    wide = HEADS_STEP * HEAD_DIM
    steps = feats // wide
    me = lax.axis_index("seq")
    last = shards - 1
    prior, following = jnp.maximum(me - 1, 0), jnp.minimum(me + 1, last)
    lead = lax.rem(me * rows + OFF, BLOCK)
    lead_next = lax.rem((me + 1) * rows + OFF, BLOCK)
    ways = ((TAIL, lambda x: x > OFF), (OFF, lambda x: x <= OFF))

    slot_ref[...] = jnp.zeros_like(slot_ref)
    got_ref[...] = jnp.zeros_like(got_ref)
    halo_ref[...] = jnp.zeros_like(halo_ref)
    after_ref[...] = jnp.zeros_like(after_ref)
    slot_ref[me] = mine_ref[...]

    barrier = pltpu.get_barrier_semaphore()

    def greet(p, carry):
        @pl.when(p != me)
        def _():
            pl.semaphore_signal(
                barrier, inc=1, device_id={"seq": p}, device_id_type=pl.DeviceIdType.MESH
            )
        return carry

    lax.fori_loop(0, shards, greet, 0)
    pl.semaphore_wait(barrier, shards - 1)

    def halo_copy(i, size):
        return remote(
            (k_ref, v_ref)[i].at[pl.ds(rows - size, size)],
            halo_ref.at[i, pl.ds(TAIL - size, size)],
            halo_send.at[i], halo_recv.at[i], following,
        )

    def back_copy(j, size):
        part = (slice(None), pl.ds(TAIL - size, size), pl.ds(pl.multiple_of(j * wide, wide), wide))
        return remote(
            hg_ref.at[part], after_ref.at[part], back_send.at[j], back_recv.at[j], prior
        )

    def slot_copy(p, owner):
        return remote(mine_ref, slot_ref.at[owner], slot_send.at[p], slot_recv.at[owner], p)

    def part_copy(p, sender):
        return remote(part_ref.at[p], got_ref.at[sender], part_send.at[p], part_recv.at[sender], p)

    def each(low, high, action):
        def step(p, carry):
            action(p)
            return carry
        lax.fori_loop(low, high, step, 0)

    for size, fits in ways:
        @pl.when((me < last) & fits(lead_next))
        def _():
            for i in range(2):
                halo_copy(i, size).start()
    each(me + 1, shards, lambda p: slot_copy(p, me).start())

    local, summary = bias_of(me, rows, slots)
    bias_ref[:, : TAIL + rows] = local
    bias_ref[:, TAIL + rows :] = summary

    for size, fits in ways:
        @pl.when((me > 0) & fits(lead))
        def _():
            for i in range(2):
                halo_copy(i, size).wait_recv()
    each(0, me, lambda p: slot_copy(p, p).wait_recv())

    ks_ref[...] = slot_ref[:, :half].astype(jnp.float32).reshape(shards * half, HEAD_DIM)
    vs_ref[...] = slot_ref[:, half:].astype(jnp.float32).reshape(shards * half, HEAD_DIM)

    def group(j, carry):
        for i in range(HEADS_STEP):
            h = j * HEADS_STEP + i
            c = pl.ds(pl.multiple_of(h * HEAD_DIM, HEAD_DIM), HEAD_DIM)
            of_head = pl.ds(h, slots, stride=HEADS)
            k_slots = ks_ref[of_head, :].astype(jnp.bfloat16)
            v_slots = vs_ref[of_head, :].astype(jnp.bfloat16)
            k = jnp.concatenate([halo_ref[0, :, c], k_ref[:, c], k_slots], axis=0)
            v = jnp.concatenate([halo_ref[1, :, c], v_ref[:, c], v_slots], axis=0)
            attended, qgrad, kg, vg = one_head(q_ref[:, c], k, v, g_ref[:, c], bias_ref[...])
            out_ref[:, c] = attended
            qg_ref[:, c] = qgrad
            for n, (grad, own_ref, term_ref) in enumerate(((kg, kg_ref, kp_ref), (vg, vg_ref, vp_ref))):
                hg_ref[n, :, c] = grad[:TAIL].astype(jnp.bfloat16)
                own_ref[:, c] = grad[TAIL : TAIL + rows]
                term_ref[of_head, :] = grad[TAIL + rows :]
        for size, fits in ways:
            @pl.when((me > 0) & fits(lead))
            def _():
                back_copy(j, size).start()
        return carry

    lax.fori_loop(0, steps, group, 0)

    part_ref[:, :half] = kp_ref[...].astype(jnp.bfloat16).reshape(shards, half, HEAD_DIM)
    part_ref[:, half:] = vp_ref[...].astype(jnp.bfloat16).reshape(shards, half, HEAD_DIM)
    each(0, me, lambda p: part_copy(p, me).start())
    got_ref[me] = part_ref[me]
    for size, fits in ways:
        @pl.when((me < last) & fits(lead_next))
        def _():
            each(0, steps, lambda j: back_copy(j, size).wait_recv())
    each(me + 1, shards, lambda p: part_copy(p, p).wait_recv())
    sum_ref[...] = jnp.sum(got_ref[...].astype(jnp.float32), axis=0)

    for size, fits in ways:
        @pl.when((me < last) & fits(lead_next))
        def _():
            for i in range(2):
                halo_copy(i, size).wait_send()

        @pl.when((me > 0) & fits(lead))
        def _():
            each(0, steps, lambda j: back_copy(j, size).wait_send())
    each(me + 1, shards, lambda p: slot_copy(p, me).wait_send())
    each(0, me, lambda p: part_copy(p, me).wait_send())


def attention(query_rows, key_rows, value_rows, out_grad, own_slots):
    rows, feats = query_rows.shape
    shards = lax.axis_size("seq")
    slots = shards * SLOT_DEV
    half = SLOT_DEV * HEADS
    columns = TAIL + rows + slots
    steps = feats // (HEADS_STEP * HEAD_DIM)
    vmem = pl.BlockSpec(memory_space=pltpu.VMEM)
    bf16, f32 = jnp.bfloat16, jnp.float32
    return pl.pallas_call(
        functools.partial(kernel, shards),
        in_specs=[vmem] * 5,
        out_specs=[vmem] * 6,
        out_shape=[
            jax.ShapeDtypeStruct((rows, feats), bf16),
            jax.ShapeDtypeStruct((rows, feats), bf16),
            jax.ShapeDtypeStruct((rows, feats), f32),
            jax.ShapeDtypeStruct((rows, feats), f32),
            jax.ShapeDtypeStruct((2, TAIL, feats), bf16),
            jax.ShapeDtypeStruct((2 * half, HEAD_DIM), f32),
        ],
        scratch_shapes=[
            pltpu.VMEM((rows, columns), f32),
            pltpu.VMEM((2, TAIL, feats), bf16),
            pltpu.VMEM((2, TAIL, feats), bf16),
            pltpu.VMEM((shards, 2 * half, HEAD_DIM), bf16),
            pltpu.VMEM((shards, 2 * half, HEAD_DIM), bf16),
            pltpu.VMEM((shards, 2 * half, HEAD_DIM), bf16),
            pltpu.VMEM((shards * half, HEAD_DIM), f32),
            pltpu.VMEM((shards * half, HEAD_DIM), f32),
            pltpu.VMEM((shards * half, HEAD_DIM), f32),
            pltpu.VMEM((shards * half, HEAD_DIM), f32),
            pltpu.SemaphoreType.DMA((2,)),
            pltpu.SemaphoreType.DMA((2,)),
            pltpu.SemaphoreType.DMA((shards,)),
            pltpu.SemaphoreType.DMA((shards,)),
            pltpu.SemaphoreType.DMA((steps,)),
            pltpu.SemaphoreType.DMA((steps,)),
            pltpu.SemaphoreType.DMA((shards,)),
            pltpu.SemaphoreType.DMA((shards,)),
        ],
        compiler_params=pltpu.CompilerParams(
            vmem_limit_bytes=48 * 1024 * 1024, collective_id=0, has_side_effects=True
        ),
        cost_estimate=pl.CostEstimate(
            flops=10 * rows * columns * feats,
            bytes_accessed=24 * rows * feats,
            transcendentals=HEADS * rows * columns,
        ),
    )(query_rows, key_rows, value_rows, out_grad, own_slots)


def body(query_rows, key_rows, value_rows, out_grad):
    rows, feats = query_rows.shape
    shard = lax.axis_index("seq")
    lead = (shard * rows + OFF) % BLOCK
    index = [BLOCK - 1 - lead + BLOCK * i for i in range(SLOT_DEV)]
    own_slots = jnp.stack([
        jnp.concatenate([
            jnp.where(i < rows, lax.dynamic_slice_in_dim(array, jnp.minimum(i, rows - 1), 1, 0), 0)
            for i in index
        ])
        for array in (key_rows, value_rows)
    ])
    attended, query_grad, key_own, value_own, after, terms = attention(
        query_rows, key_rows, value_rows, out_grad, own_slots.reshape(-1, HEAD_DIM)
    )
    mine = terms.reshape(2, SLOT_DEV, feats)
    row = jnp.arange(rows, dtype=jnp.int32)[:, None]

    def total(own, i):
        grad = own + jnp.pad(after[i].astype(jnp.float32), ((rows - TAIL, 0), (0, 0)))
        for s in range(SLOT_DEV):
            grad = grad + jnp.where(row == index[s], mine[i, s][None, :], 0.0)
        return grad.astype(jnp.bfloat16)

    return attended, query_grad, total(key_own, 0), total(value_own, 1)


def solution(mesh):
    spec = P(("groups", "seq"), None)
    return jax.shard_map(
        body, mesh=mesh, in_specs=(spec,) * 4, out_specs=(spec,) * 4, check_vma=False
    )
```

```python
import functools
import math

import jax
import jax.numpy as jnp
from jax import lax
from jax.experimental import pallas as pl
from jax.experimental.pallas import tpu as pltpu
from jax.sharding import PartitionSpec as P

HEADS = 16
HEAD_DIM = 128
BLOCK = 128
OFF = 32
TAIL = 96
SLOT_DEV = 2
HEADS_STEP = 4
SCALE = 1.0 / math.sqrt(HEAD_DIM)
NEG = -1e30


def bias_of(shard, rows, slots):
    first = shard * rows
    shape = (rows, TAIL + rows)
    query = first + lax.broadcasted_iota(jnp.int32, shape, 0)
    pos = first - TAIL + lax.broadcasted_iota(jnp.int32, shape, 1)
    local = (pos >= 0) & (pos <= query) & ((pos + OFF) >> 7 == (query + OFF) >> 7)
    shape = (rows, slots)
    query = first + lax.broadcasted_iota(jnp.int32, shape, 0)
    slot = lax.broadcasted_iota(jnp.int32, shape, 1)
    start = (slot >> 1) * rows
    offset = BLOCK - 1 - ((start + OFF) & (BLOCK - 1)) + BLOCK * (slot & 1)
    summary = (offset < rows) & ((start + offset + OFF) >> 7 < (query + OFF) >> 7)
    return (
        jnp.where(local, 0.0, NEG).astype(jnp.float32),
        jnp.where(summary, 0.0, NEG).astype(jnp.float32),
    )


def dot(a, b, dims):
    return lax.dot_general(a, b, (dims, ((), ())), preferred_element_type=jnp.float32)


NT = ((1,), (1,))
NN = ((1,), (0,))
TN = ((0,), (0,))


def one_head(q, k, v, g, bias):
    scores = dot(q, k, NT) * SCALE + bias
    top = jnp.max(scores, axis=1, keepdims=True)
    expo = jnp.exp(scores - top)
    prob = expo * (1.0 / jnp.sum(expo, axis=1, keepdims=True))
    weights = prob.astype(jnp.bfloat16)
    attended = dot(weights, v, NN).astype(jnp.bfloat16)
    delta = jnp.sum(g.astype(jnp.float32) * attended.astype(jnp.float32), axis=1, keepdims=True)
    dscores = (prob * (dot(g, v, NT) - delta)).astype(jnp.bfloat16)
    qgrad = (dot(dscores, k, NN) * SCALE).astype(jnp.bfloat16)
    return attended, qgrad, dot(dscores, q, TN) * SCALE, dot(weights, g, TN)


def remote(src, dst, send, recv, seq):
    return pltpu.make_async_remote_copy(
        src_ref=src, dst_ref=dst, send_sem=send, recv_sem=recv,
        device_id={"seq": seq}, device_id_type=pl.DeviceIdType.MESH,
    )


def kernel(shards, q_in, k_in, v_in, g_in, mine_ref, out_ref, qg_ref, key_ref, value_ref,
           q_ref, k_ref, v_ref, g_ref, kg_ref, vg_ref, after_ref, sum_ref, bias_ref, halo_ref, hg_ref, slot_ref, part_ref, got_ref, ks_ref, vs_ref,
           kp_ref, vp_ref, halo_send, halo_recv, slot_send, slot_recv, back_send, back_recv,
           part_send, part_recv, load_sem):
    rows, feats = q_ref.shape
    slots = shards * SLOT_DEV
    half = SLOT_DEV * HEADS
    wide = HEADS_STEP * HEAD_DIM
    steps = feats // wide
    me = lax.axis_index("seq")
    last = shards - 1
    prior, following = jnp.maximum(me - 1, 0), jnp.minimum(me + 1, last)
    lead = lax.rem(me * rows + OFF, BLOCK)
    lead_next = lax.rem((me + 1) * rows + OFF, BLOCK)
    ways = ((TAIL, lambda x: x > OFF), (OFF, lambda x: x <= OFF))

    loads = [
        pltpu.make_async_copy(source, target, load_sem.at[i])
        for i, (source, target) in enumerate(
            ((q_in, q_ref), (k_in, k_ref), (v_in, v_ref), (g_in, g_ref))
        )
    ]
    for load in loads:
        load.start()

    slot_ref[...] = jnp.zeros_like(slot_ref)
    got_ref[...] = jnp.zeros_like(got_ref)
    short = jnp.zeros((2, TAIL - OFF, feats), jnp.bfloat16)
    rest = jnp.zeros((2, OFF, feats), jnp.bfloat16)
    for ref, missing, alone in ((halo_ref, lead <= OFF, me == 0), (after_ref, lead_next <= OFF, me == last)):
        @pl.when(missing | alone)
        def _():
            ref[:, : TAIL - OFF] = short

        @pl.when(alone)
        def _():
            ref[:, TAIL - OFF :] = rest
    slot_ref[me] = mine_ref[...]

    barrier = pltpu.get_barrier_semaphore()

    def greet(p, carry):
        @pl.when(p != me)
        def _():
            pl.semaphore_signal(
                barrier, inc=1, device_id={"seq": p}, device_id_type=pl.DeviceIdType.MESH
            )
        return carry

    lax.fori_loop(0, shards, greet, 0)
    pl.semaphore_wait(barrier, shards - 1)

    def halo_copy(i, j, size):
        cols = pl.ds(pl.multiple_of(j * wide, wide), wide)
        return remote(
            (k_in, v_in)[i].at[pl.ds(rows - size, size), cols],
            halo_ref.at[i, pl.ds(TAIL - size, size), cols],
            halo_send.at[i, j], halo_recv.at[i, j], following,
        )

    def back_copy(j, size):
        part = (slice(None), pl.ds(TAIL - size, size), pl.ds(pl.multiple_of(j * wide, wide), wide))
        return remote(
            hg_ref.at[part], after_ref.at[part], back_send.at[j], back_recv.at[j], prior
        )

    def slot_copy(p, owner):
        return remote(mine_ref, slot_ref.at[owner], slot_send.at[p], slot_recv.at[owner], p)

    def part_copy(p, sender):
        return remote(part_ref.at[p], got_ref.at[sender], part_send.at[p], part_recv.at[sender], p)

    def each(low, high, action):
        def step(p, carry):
            action(p)
            return carry
        lax.fori_loop(low, high, step, 0)

    each(me + 1, shards, lambda p: slot_copy(p, me).start())
    for size, fits in ways:
        @pl.when((me < last) & fits(lead_next))
        def _():
            def send(j):
                for i in range(2):
                    halo_copy(i, j, size).start()
            each(0, steps, send)

    local, summary = bias_of(me, rows, slots)
    bias_ref[:, : TAIL + rows] = local
    bias_ref[:, TAIL + rows :] = summary

    each(0, me, lambda p: slot_copy(p, p).wait_recv())

    ks_ref[...] = slot_ref[:, :half].astype(jnp.float32).reshape(shards * half, HEAD_DIM)
    vs_ref[...] = slot_ref[:, half:].astype(jnp.float32).reshape(shards * half, HEAD_DIM)

    for load in loads:
        load.wait()

    def group(j, carry):
        for size, fits in ways:
            @pl.when((me > 0) & fits(lead))
            def _():
                for i in range(2):
                    halo_copy(i, j, size).wait_recv()
        for i in range(HEADS_STEP):
            h = j * HEADS_STEP + i
            c = pl.ds(pl.multiple_of(h * HEAD_DIM, HEAD_DIM), HEAD_DIM)
            of_head = pl.ds(h, slots, stride=HEADS)
            k_slots = ks_ref[of_head, :].astype(jnp.bfloat16)
            v_slots = vs_ref[of_head, :].astype(jnp.bfloat16)
            k = jnp.concatenate([halo_ref[0, :, c], k_ref[:, c], k_slots], axis=0)
            v = jnp.concatenate([halo_ref[1, :, c], v_ref[:, c], v_slots], axis=0)
            attended, qgrad, kg, vg = one_head(q_ref[:, c], k, v, g_ref[:, c], bias_ref[...])
            out_ref[:, c] = attended
            qg_ref[:, c] = qgrad
            for n, (grad, own_ref, term_ref) in enumerate(((kg, kg_ref, kp_ref), (vg, vg_ref, vp_ref))):
                hg_ref[n, :, c] = grad[:TAIL].astype(jnp.bfloat16)
                own_ref[:, c] = grad[TAIL : TAIL + rows]
                term_ref[of_head, :] = grad[TAIL + rows :]
        for size, fits in ways:
            @pl.when((me > 0) & fits(lead))
            def _():
                back_copy(j, size).start()
        return carry

    lax.fori_loop(0, steps, group, 0)

    part_ref[:, :half] = kp_ref[...].astype(jnp.bfloat16).reshape(shards, half, HEAD_DIM)
    part_ref[:, half:] = vp_ref[...].astype(jnp.bfloat16).reshape(shards, half, HEAD_DIM)
    each(0, me, lambda p: part_copy(p, me).start())
    got_ref[me] = part_ref[me]
    for size, fits in ways:
        @pl.when((me < last) & fits(lead_next))
        def _():
            each(0, steps, lambda j: back_copy(j, size).wait_recv())
    grads = ((kg_ref, key_ref), (vg_ref, value_ref))
    for n, (own_ref, _) in enumerate(grads):
        own_ref[rows - TAIL :] += after_ref[n].astype(jnp.float32)
    each(me + 1, shards, lambda p: part_copy(p, p).wait_recv())
    sum_ref[...] = jnp.sum(got_ref[...].astype(jnp.float32), axis=0)
    for t in range(SLOT_DEV):
        index = BLOCK - 1 - lead + BLOCK * t

        @pl.when(index < rows)
        def _():
            at = pl.ds(pl.multiple_of(jnp.minimum(index, rows - 1) - 7, 8), 8)
            ends = lax.broadcasted_iota(jnp.int32, (8, HEAD_DIM), 0) == 7
            for n, (own_ref, _) in enumerate(grads):
                for h in range(HEADS):
                    c = slice(h * HEAD_DIM, (h + 1) * HEAD_DIM)
                    r = (n * SLOT_DEV + t) * HEADS + h
                    own_ref[at, c] += jnp.where(ends, sum_ref[r : r + 1, :], 0.0)
    for own_ref, final_ref in grads:
        final_ref[...] = own_ref[...].astype(jnp.bfloat16)

    for size, fits in ways:
        @pl.when((me < last) & fits(lead_next))
        def _():
            def sent(j):
                for i in range(2):
                    halo_copy(i, j, size).wait_send()
            each(0, steps, sent)

        @pl.when((me > 0) & fits(lead))
        def _():
            each(0, steps, lambda j: back_copy(j, size).wait_send())
    each(me + 1, shards, lambda p: slot_copy(p, me).wait_send())
    each(0, me, lambda p: part_copy(p, me).wait_send())


def attention(query_rows, key_rows, value_rows, out_grad, own_slots):
    rows, feats = query_rows.shape
    shards = lax.axis_size("seq")
    slots = shards * SLOT_DEV
    half = SLOT_DEV * HEADS
    columns = TAIL + rows + slots
    steps = feats // (HEADS_STEP * HEAD_DIM)
    vmem = pl.BlockSpec(memory_space=pltpu.VMEM)
    bf16, f32 = jnp.bfloat16, jnp.float32
    return pl.pallas_call(
        functools.partial(kernel, shards),
        in_specs=[pl.BlockSpec(memory_space=pl.ANY)] * 4 + [vmem],
        out_specs=[vmem] * 4,
        out_shape=[jax.ShapeDtypeStruct((rows, feats), bf16)] * 4,
        scratch_shapes=[
            pltpu.VMEM((rows, feats), bf16),
            pltpu.VMEM((rows, feats), bf16),
            pltpu.VMEM((rows, feats), bf16),
            pltpu.VMEM((rows, feats), bf16),
            pltpu.VMEM((rows, feats), f32),
            pltpu.VMEM((rows, feats), f32),
            pltpu.VMEM((2, TAIL, feats), bf16),
            pltpu.VMEM((2 * half, HEAD_DIM), f32),
            pltpu.VMEM((rows, columns), f32),
            pltpu.VMEM((2, TAIL, feats), bf16),
            pltpu.VMEM((2, TAIL, feats), bf16),
            pltpu.VMEM((shards, 2 * half, HEAD_DIM), bf16),
            pltpu.VMEM((shards, 2 * half, HEAD_DIM), bf16),
            pltpu.VMEM((shards, 2 * half, HEAD_DIM), bf16),
            pltpu.VMEM((shards * half, HEAD_DIM), f32),
            pltpu.VMEM((shards * half, HEAD_DIM), f32),
            pltpu.VMEM((shards * half, HEAD_DIM), f32),
            pltpu.VMEM((shards * half, HEAD_DIM), f32),
            pltpu.SemaphoreType.DMA((2, steps)),
            pltpu.SemaphoreType.DMA((2, steps)),
            pltpu.SemaphoreType.DMA((shards,)),
            pltpu.SemaphoreType.DMA((shards,)),
            pltpu.SemaphoreType.DMA((steps,)),
            pltpu.SemaphoreType.DMA((steps,)),
            pltpu.SemaphoreType.DMA((shards,)),
            pltpu.SemaphoreType.DMA((shards,)),
            pltpu.SemaphoreType.DMA((4,)),
        ],
        compiler_params=pltpu.CompilerParams(
            vmem_limit_bytes=56 * 1024 * 1024, collective_id=0, has_side_effects=True
        ),
        cost_estimate=pl.CostEstimate(
            flops=10 * rows * columns * feats,
            bytes_accessed=24 * rows * feats,
            transcendentals=HEADS * rows * columns,
        ),
    )(query_rows, key_rows, value_rows, out_grad, own_slots)


def body(query_rows, key_rows, value_rows, out_grad):
    rows, feats = query_rows.shape
    shard = lax.axis_index("seq")
    lead = (shard * rows + OFF) % BLOCK
    index = [BLOCK - 1 - lead + BLOCK * i for i in range(SLOT_DEV)]
    own_slots = jnp.stack([
        jnp.concatenate([
            jnp.where(i < rows, lax.dynamic_slice_in_dim(array, jnp.minimum(i, rows - 1), 1, 0), 0)
            for i in index
        ])
        for array in (key_rows, value_rows)
    ])
    return tuple(
        attention(query_rows, key_rows, value_rows, out_grad, own_slots.reshape(-1, HEAD_DIM))
    )


def solution(mesh):
    spec = P(("groups", "seq"), None)
    return jax.shard_map(
        body, mesh=mesh, in_specs=(spec,) * 4, out_specs=(spec,) * 4, check_vma=False
    )
```

```python
import functools
import math

import jax
import jax.numpy as jnp
from jax import lax
from jax.experimental import pallas as pl
from jax.experimental.pallas import tpu as pltpu
from jax.sharding import PartitionSpec as P

HEADS = 16
HEAD_DIM = 128
BLOCK = 128
OFF = 32
TAIL = 96
SLOT_DEV = 2
HEADS_STEP = 4
SCALE = 1.0 / math.sqrt(HEAD_DIM)
NEG = -1e30


def bias_of(shard, rows, slots):
    first = shard * rows
    shape = (rows, TAIL + rows)
    query = first + lax.broadcasted_iota(jnp.int32, shape, 0)
    pos = first - TAIL + lax.broadcasted_iota(jnp.int32, shape, 1)
    local = (pos >= 0) & (pos <= query) & ((pos + OFF) >> 7 == (query + OFF) >> 7)
    shape = (rows, slots)
    query = first + lax.broadcasted_iota(jnp.int32, shape, 0)
    slot = lax.broadcasted_iota(jnp.int32, shape, 1)
    start = (slot >> 1) * rows
    offset = BLOCK - 1 - ((start + OFF) & (BLOCK - 1)) + BLOCK * (slot & 1)
    summary = (offset < rows) & ((start + offset + OFF) >> 7 < (query + OFF) >> 7)
    return (
        jnp.where(local, 0.0, NEG).astype(jnp.float32),
        jnp.where(summary, 0.0, NEG).astype(jnp.float32),
    )


def dot(a, b, dims):
    return lax.dot_general(a, b, (dims, ((), ())), preferred_element_type=jnp.float32)


NT = ((1,), (1,))
NN = ((1,), (0,))
TN = ((0,), (0,))


def one_head(q, k, v, g, bias):
    scores = dot(q, k, NT) * SCALE + bias
    top = jnp.max(scores, axis=1, keepdims=True)
    expo = jnp.exp(scores - top)
    prob = expo * (1.0 / jnp.sum(expo, axis=1, keepdims=True))
    weights = prob.astype(jnp.bfloat16)
    attended = dot(weights, v, NN).astype(jnp.bfloat16)
    delta = jnp.sum(g.astype(jnp.float32) * attended.astype(jnp.float32), axis=1, keepdims=True)
    dscores = (prob * (dot(g, v, NT) - delta)).astype(jnp.bfloat16)
    qgrad = (dot(dscores, k, NN) * SCALE).astype(jnp.bfloat16)
    return attended, qgrad, dot(dscores, q, TN) * SCALE, dot(weights, g, TN)


def remote(src, dst, send, recv, seq):
    return pltpu.make_async_remote_copy(
        src_ref=src, dst_ref=dst, send_sem=send, recv_sem=recv,
        device_id={"seq": seq}, device_id_type=pl.DeviceIdType.MESH,
    )


def kernel(shards, q_in, k_in, v_in, g_in, mine_ref, out_ref, qg_ref, key_ref, value_ref,
           q_ref, k_ref, v_ref, g_ref, kg_ref, vg_ref, after_ref, sum_ref, bias_ref, halo_ref, hg_ref, slot_ref, part_ref, got_ref, ks_ref, vs_ref,
           kp_ref, vp_ref, halo_send, halo_recv, slot_send, slot_recv, back_send, back_recv,
           part_send, part_recv, load_sem):
    rows, feats = q_ref.shape
    slots = shards * SLOT_DEV
    half = SLOT_DEV * HEADS
    wide = HEADS_STEP * HEAD_DIM
    steps = feats // wide
    me = lax.axis_index("seq")
    last = shards - 1
    prior, following = jnp.maximum(me - 1, 0), jnp.minimum(me + 1, last)
    lead = lax.rem(me * rows + OFF, BLOCK)
    lead_next = lax.rem((me + 1) * rows + OFF, BLOCK)
    ways = ((TAIL, lambda x: x > OFF), (OFF, lambda x: x <= OFF))

    loads = [
        pltpu.make_async_copy(source, target, load_sem.at[i])
        for i, (source, target) in enumerate(
            ((q_in, q_ref), (k_in, k_ref), (v_in, v_ref), (g_in, g_ref))
        )
    ]
    for load in loads:
        load.start()

    slot_ref[...] = jnp.zeros_like(slot_ref)
    got_ref[...] = jnp.zeros_like(got_ref)
    short = jnp.zeros((2, TAIL - OFF, feats), jnp.bfloat16)
    rest = jnp.zeros((2, OFF, feats), jnp.bfloat16)
    for ref, missing, alone in ((halo_ref, lead <= OFF, me == 0), (after_ref, lead_next <= OFF, me == last)):
        @pl.when(missing | alone)
        def _():
            ref[:, : TAIL - OFF] = short

        @pl.when(alone)
        def _():
            ref[:, TAIL - OFF :] = rest
    slot_ref[me] = mine_ref[...]

    barrier = pltpu.get_barrier_semaphore()

    def greet(p, carry):
        @pl.when(p != me)
        def _():
            pl.semaphore_signal(
                barrier, inc=1, device_id={"seq": p}, device_id_type=pl.DeviceIdType.MESH
            )
        return carry

    lax.fori_loop(0, shards, greet, 0)
    pl.semaphore_wait(barrier, shards - 1)

    def halo_copy(i, j, size):
        cols = pl.ds(pl.multiple_of(j * wide, wide), wide)
        return remote(
            (k_in, v_in)[i].at[pl.ds(rows - size, size), cols],
            halo_ref.at[i, pl.ds(TAIL - size, size), cols],
            halo_send.at[i, j], halo_recv.at[i, j], following,
        )

    def back_copy(j, size):
        part = (slice(None), pl.ds(TAIL - size, size), pl.ds(pl.multiple_of(j * wide, wide), wide))
        return remote(
            hg_ref.at[part], after_ref.at[part], back_send.at[j], back_recv.at[j], prior
        )

    def slot_copy(p, owner):
        return remote(mine_ref, slot_ref.at[owner], slot_send.at[p], slot_recv.at[owner], p)

    def part_copy(p, sender):
        return remote(part_ref.at[p], got_ref.at[sender], part_send.at[p], part_recv.at[sender], p)

    def each(low, high, action):
        def step(p, carry):
            action(p)
            return carry
        lax.fori_loop(low, high, step, 0)

    each(me + 1, shards, lambda p: slot_copy(p, me).start())
    for size, fits in ways:
        @pl.when((me < last) & fits(lead_next))
        def _():
            def send(j):
                for i in range(2):
                    halo_copy(i, j, size).start()
            each(0, steps, send)

    local, summary = bias_of(me, rows, slots)
    bias_ref[:, : TAIL + rows] = local
    bias_ref[:, TAIL + rows :] = summary

    each(0, me, lambda p: slot_copy(p, p).wait_recv())

    ks_ref[...] = slot_ref[:, :half].astype(jnp.float32).reshape(shards * half, HEAD_DIM)
    vs_ref[...] = slot_ref[:, half:].astype(jnp.float32).reshape(shards * half, HEAD_DIM)

    for load in loads:
        load.wait()

    def group(j, carry):
        for size, fits in ways:
            @pl.when((me > 0) & fits(lead))
            def _():
                for i in range(2):
                    halo_copy(i, j, size).wait_recv()
        for i in range(HEADS_STEP):
            h = j * HEADS_STEP + i
            c = pl.ds(pl.multiple_of(h * HEAD_DIM, HEAD_DIM), HEAD_DIM)
            of_head = pl.ds(h, slots, stride=HEADS)
            k_slots = ks_ref[of_head, :].astype(jnp.bfloat16)
            v_slots = vs_ref[of_head, :].astype(jnp.bfloat16)
            k = jnp.concatenate([halo_ref[0, :, c], k_ref[:, c], k_slots], axis=0)
            v = jnp.concatenate([halo_ref[1, :, c], v_ref[:, c], v_slots], axis=0)
            attended, qgrad, kg, vg = one_head(q_ref[:, c], k, v, g_ref[:, c], bias_ref[...])
            out_ref[:, c] = attended
            qg_ref[:, c] = qgrad
            for n, (grad, own_ref, term_ref) in enumerate(((kg, kg_ref, kp_ref), (vg, vg_ref, vp_ref))):
                hg_ref[n, :, c] = grad[:TAIL].astype(jnp.bfloat16)
                own_ref[:, c] = grad[TAIL : TAIL + rows]
                term_ref[of_head, :] = grad[TAIL + rows :]
        for size, fits in ways:
            @pl.when((me > 0) & fits(lead))
            def _():
                back_copy(j, size).start()
        return carry

    lax.fori_loop(0, steps, group, 0)

    part_ref[:, :half] = kp_ref[...].astype(jnp.bfloat16).reshape(shards, half, HEAD_DIM)
    part_ref[:, half:] = vp_ref[...].astype(jnp.bfloat16).reshape(shards, half, HEAD_DIM)
    each(0, me, lambda p: part_copy(p, me).start())
    got_ref[me] = part_ref[me]
    for size, fits in ways:
        @pl.when((me < last) & fits(lead_next))
        def _():
            each(0, steps, lambda j: back_copy(j, size).wait_recv())
    grads = ((kg_ref, key_ref), (vg_ref, value_ref))
    for n, (own_ref, _) in enumerate(grads):
        own_ref[rows - TAIL :] += after_ref[n].astype(jnp.float32)
    each(me + 1, shards, lambda p: part_copy(p, p).wait_recv())
    sum_ref[...] = jnp.sum(got_ref[...].astype(jnp.float32), axis=0)
    for t in range(SLOT_DEV):
        index = BLOCK - 1 - lead + BLOCK * t

        @pl.when(index < rows)
        def _():
            at = pl.ds(pl.multiple_of(jnp.minimum(index, rows - 1) - 7, 8), 8)
            ends = lax.broadcasted_iota(jnp.int32, (8, HEAD_DIM), 0) == 7
            for n, (own_ref, _) in enumerate(grads):
                for h in range(HEADS):
                    c = slice(h * HEAD_DIM, (h + 1) * HEAD_DIM)
                    r = (n * SLOT_DEV + t) * HEADS + h
                    own_ref[at, c] += jnp.where(ends, sum_ref[r : r + 1, :], 0.0)
    for own_ref, final_ref in grads:
        final_ref[...] = own_ref[...].astype(jnp.bfloat16)

    for size, fits in ways:
        @pl.when((me < last) & fits(lead_next))
        def _():
            def sent(j):
                for i in range(2):
                    halo_copy(i, j, size).wait_send()
            each(0, steps, sent)

        @pl.when((me > 0) & fits(lead))
        def _():
            each(0, steps, lambda j: back_copy(j, size).wait_send())
    each(me + 1, shards, lambda p: slot_copy(p, me).wait_send())
    each(0, me, lambda p: part_copy(p, me).wait_send())


def attention(query_rows, key_rows, value_rows, out_grad, own_slots):
    rows, feats = query_rows.shape
    shards = lax.axis_size("seq")
    slots = shards * SLOT_DEV
    half = SLOT_DEV * HEADS
    columns = TAIL + rows + slots
    steps = feats // (HEADS_STEP * HEAD_DIM)
    vmem = pl.BlockSpec(memory_space=pltpu.VMEM)
    bf16, f32 = jnp.bfloat16, jnp.float32
    return pl.pallas_call(
        functools.partial(kernel, shards),
        in_specs=[pl.BlockSpec(memory_space=pltpu.HBM)] * 4 + [vmem],
        out_specs=[vmem] * 4,
        out_shape=[jax.ShapeDtypeStruct((rows, feats), bf16)] * 4,
        scratch_shapes=[
            pltpu.VMEM((rows, feats), bf16),
            pltpu.VMEM((rows, feats), bf16),
            pltpu.VMEM((rows, feats), bf16),
            pltpu.VMEM((rows, feats), bf16),
            pltpu.VMEM((rows, feats), f32),
            pltpu.VMEM((rows, feats), f32),
            pltpu.VMEM((2, TAIL, feats), bf16),
            pltpu.VMEM((2 * half, HEAD_DIM), f32),
            pltpu.VMEM((rows, columns), f32),
            pltpu.VMEM((2, TAIL, feats), bf16),
            pltpu.VMEM((2, TAIL, feats), bf16),
            pltpu.VMEM((shards, 2 * half, HEAD_DIM), bf16),
            pltpu.VMEM((shards, 2 * half, HEAD_DIM), bf16),
            pltpu.VMEM((shards, 2 * half, HEAD_DIM), bf16),
            pltpu.VMEM((shards * half, HEAD_DIM), f32),
            pltpu.VMEM((shards * half, HEAD_DIM), f32),
            pltpu.VMEM((shards * half, HEAD_DIM), f32),
            pltpu.VMEM((shards * half, HEAD_DIM), f32),
            pltpu.SemaphoreType.DMA((2, steps)),
            pltpu.SemaphoreType.DMA((2, steps)),
            pltpu.SemaphoreType.DMA((shards,)),
            pltpu.SemaphoreType.DMA((shards,)),
            pltpu.SemaphoreType.DMA((steps,)),
            pltpu.SemaphoreType.DMA((steps,)),
            pltpu.SemaphoreType.DMA((shards,)),
            pltpu.SemaphoreType.DMA((shards,)),
            pltpu.SemaphoreType.DMA((4,)),
        ],
        compiler_params=pltpu.CompilerParams(
            vmem_limit_bytes=51 * 1024 * 1024, collective_id=0, has_side_effects=True
        ),
        cost_estimate=pl.CostEstimate(
            flops=10 * rows * columns * feats,
            bytes_accessed=24 * rows * feats,
            transcendentals=HEADS * rows * columns,
        ),
    )(query_rows, key_rows, value_rows, out_grad, own_slots)


def body(query_rows, key_rows, value_rows, out_grad):
    rows, feats = query_rows.shape
    shard = lax.axis_index("seq")
    lead = (shard * rows + OFF) % BLOCK
    index = [BLOCK - 1 - lead + BLOCK * i for i in range(SLOT_DEV)]
    own_slots = jnp.stack([
        jnp.concatenate([
            jnp.where(i < rows, lax.dynamic_slice_in_dim(array, jnp.minimum(i, rows - 1), 1, 0), 0)
            for i in index
        ])
        for array in (key_rows, value_rows)
    ])
    return tuple(
        attention(query_rows, key_rows, value_rows, out_grad, own_slots.reshape(-1, HEAD_DIM))
    )


def solution(mesh):
    spec = P(("groups", "seq"), None)
    return jax.shard_map(
        body, mesh=mesh, in_specs=(spec,) * 4, out_specs=(spec,) * 4, check_vma=False
    )
```

```python
import functools
import math

import jax
import jax.numpy as jnp
from jax import lax
from jax.experimental import pallas as pl
from jax.experimental.pallas import tpu as pltpu
from jax.sharding import PartitionSpec as P

HEADS = 16
HEAD_DIM = 128
BLOCK = 128
OFF = 32
TAIL = 96
SLOT_DEV = 2
HEADS_STEP = 8
SCALE = 1.0 / math.sqrt(HEAD_DIM)
NEG = -1e30


def bias_of(shard, rows, slots):
    first = shard * rows
    shape = (rows, TAIL + rows)
    query = first + lax.broadcasted_iota(jnp.int32, shape, 0)
    pos = first - TAIL + lax.broadcasted_iota(jnp.int32, shape, 1)
    local = (pos >= 0) & (pos <= query) & ((pos + OFF) >> 7 == (query + OFF) >> 7)
    shape = (rows, slots)
    query = first + lax.broadcasted_iota(jnp.int32, shape, 0)
    slot = lax.broadcasted_iota(jnp.int32, shape, 1)
    start = (slot >> 1) * rows
    offset = BLOCK - 1 - ((start + OFF) & (BLOCK - 1)) + BLOCK * (slot & 1)
    summary = (offset < rows) & ((start + offset + OFF) >> 7 < (query + OFF) >> 7)
    return (
        jnp.where(local, 0.0, NEG).astype(jnp.float32),
        jnp.where(summary, 0.0, NEG).astype(jnp.float32),
    )


def dot(a, b, dims):
    return lax.dot_general(a, b, (dims, ((), ())), preferred_element_type=jnp.float32)


NT = ((1,), (1,))
NN = ((1,), (0,))
TN = ((0,), (0,))


def one_head(q, k, v, g, bias):
    scores = dot(q, k, NT) * SCALE + bias
    top = jnp.max(scores, axis=1, keepdims=True)
    expo = jnp.exp(scores - top)
    prob = expo * (1.0 / jnp.sum(expo, axis=1, keepdims=True))
    weights = prob.astype(jnp.bfloat16)
    attended = dot(weights, v, NN).astype(jnp.bfloat16)
    delta = jnp.sum(g.astype(jnp.float32) * attended.astype(jnp.float32), axis=1, keepdims=True)
    dscores = (prob * (dot(g, v, NT) - delta)).astype(jnp.bfloat16)
    qgrad = (dot(dscores, k, NN) * SCALE).astype(jnp.bfloat16)
    return attended, qgrad, dot(dscores, q, TN) * SCALE, dot(weights, g, TN)


def remote(src, dst, send, recv, seq):
    return pltpu.make_async_remote_copy(
        src_ref=src, dst_ref=dst, send_sem=send, recv_sem=recv,
        device_id={"seq": seq}, device_id_type=pl.DeviceIdType.MESH,
    )


def kernel(shards, q_in, k_in, v_in, g_in, mine_ref, out_ref, qg_ref, key_ref, value_ref,
           q_ref, k_ref, v_ref, g_ref, kg_ref, vg_ref, after_ref, sum_ref, bias_ref, halo_ref, hg_ref, slot_ref, part_ref, got_ref, ks_ref, vs_ref,
           kp_ref, vp_ref, halo_send, halo_recv, slot_send, slot_recv, back_send, back_recv,
           part_send, part_recv, load_sem):
    rows, feats = q_ref.shape
    slots = shards * SLOT_DEV
    half = SLOT_DEV * HEADS
    wide = HEADS_STEP * HEAD_DIM
    steps = feats // wide
    me = lax.axis_index("seq")
    last = shards - 1
    prior, following = jnp.maximum(me - 1, 0), jnp.minimum(me + 1, last)
    lead = lax.rem(me * rows + OFF, BLOCK)
    lead_next = lax.rem((me + 1) * rows + OFF, BLOCK)
    ways = ((TAIL, lambda x: x > OFF), (OFF, lambda x: x <= OFF))

    loads = [
        pltpu.make_async_copy(source, target, load_sem.at[i])
        for i, (source, target) in enumerate(
            ((q_in, q_ref), (k_in, k_ref), (v_in, v_ref), (g_in, g_ref))
        )
    ]
    for load in loads:
        load.start()

    slot_ref[...] = jnp.zeros_like(slot_ref)
    got_ref[...] = jnp.zeros_like(got_ref)
    short = jnp.zeros((2, TAIL - OFF, feats), jnp.bfloat16)
    rest = jnp.zeros((2, OFF, feats), jnp.bfloat16)
    for ref, missing, alone in ((halo_ref, lead <= OFF, me == 0), (after_ref, lead_next <= OFF, me == last)):
        @pl.when(missing | alone)
        def _():
            ref[:, : TAIL - OFF] = short

        @pl.when(alone)
        def _():
            ref[:, TAIL - OFF :] = rest
    slot_ref[me] = mine_ref[...]

    barrier = pltpu.get_barrier_semaphore()

    def greet(p, carry):
        @pl.when(p != me)
        def _():
            pl.semaphore_signal(
                barrier, inc=1, device_id={"seq": p}, device_id_type=pl.DeviceIdType.MESH
            )
        return carry

    lax.fori_loop(0, shards, greet, 0)
    pl.semaphore_wait(barrier, shards - 1)

    def halo_copy(i, j, size):
        cols = pl.ds(pl.multiple_of(j * wide, wide), wide)
        return remote(
            (k_in, v_in)[i].at[pl.ds(rows - size, size), cols],
            halo_ref.at[i, pl.ds(TAIL - size, size), cols],
            halo_send.at[i, j], halo_recv.at[i, j], following,
        )

    def back_copy(j, size):
        part = (slice(None), pl.ds(TAIL - size, size), pl.ds(pl.multiple_of(j * wide, wide), wide))
        return remote(
            hg_ref.at[part], after_ref.at[part], back_send.at[j], back_recv.at[j], prior
        )

    def slot_copy(p, owner):
        return remote(mine_ref, slot_ref.at[owner], slot_send.at[p], slot_recv.at[owner], p)

    def part_copy(p, sender):
        return remote(part_ref.at[p], got_ref.at[sender], part_send.at[p], part_recv.at[sender], p)

    def each(low, high, action):
        def step(p, carry):
            action(p)
            return carry
        lax.fori_loop(low, high, step, 0)

    each(me + 1, shards, lambda p: slot_copy(p, me).start())
    for size, fits in ways:
        @pl.when((me < last) & fits(lead_next))
        def _():
            def send(j):
                for i in range(2):
                    halo_copy(i, j, size).start()
            each(0, steps, send)

    local, summary = bias_of(me, rows, slots)
    bias_ref[:, : TAIL + rows] = local
    bias_ref[:, TAIL + rows :] = summary

    each(0, me, lambda p: slot_copy(p, p).wait_recv())

    ks_ref[...] = slot_ref[:, :half].astype(jnp.float32).reshape(shards * half, HEAD_DIM)
    vs_ref[...] = slot_ref[:, half:].astype(jnp.float32).reshape(shards * half, HEAD_DIM)

    for load in loads:
        load.wait()

    def group(j, carry):
        for size, fits in ways:
            @pl.when((me > 0) & fits(lead))
            def _():
                for i in range(2):
                    halo_copy(i, j, size).wait_recv()
        for i in range(HEADS_STEP):
            h = j * HEADS_STEP + i
            c = pl.ds(pl.multiple_of(h * HEAD_DIM, HEAD_DIM), HEAD_DIM)
            of_head = pl.ds(h, slots, stride=HEADS)
            k_slots = ks_ref[of_head, :].astype(jnp.bfloat16)
            v_slots = vs_ref[of_head, :].astype(jnp.bfloat16)
            k = jnp.concatenate([halo_ref[0, :, c], k_ref[:, c], k_slots], axis=0)
            v = jnp.concatenate([halo_ref[1, :, c], v_ref[:, c], v_slots], axis=0)
            attended, qgrad, kg, vg = one_head(q_ref[:, c], k, v, g_ref[:, c], bias_ref[...])
            out_ref[:, c] = attended
            qg_ref[:, c] = qgrad
            for n, (grad, own_ref, term_ref) in enumerate(((kg, kg_ref, kp_ref), (vg, vg_ref, vp_ref))):
                hg_ref[n, :, c] = grad[:TAIL].astype(jnp.bfloat16)
                own_ref[:, c] = grad[TAIL : TAIL + rows]
                term_ref[of_head, :] = grad[TAIL + rows :]
        for size, fits in ways:
            @pl.when((me > 0) & fits(lead))
            def _():
                back_copy(j, size).start()
        return carry

    lax.fori_loop(0, steps, group, 0)

    part_ref[:, :half] = kp_ref[...].astype(jnp.bfloat16).reshape(shards, half, HEAD_DIM)
    part_ref[:, half:] = vp_ref[...].astype(jnp.bfloat16).reshape(shards, half, HEAD_DIM)
    each(0, me, lambda p: part_copy(p, me).start())
    got_ref[me] = part_ref[me]
    for size, fits in ways:
        @pl.when((me < last) & fits(lead_next))
        def _():
            each(0, steps, lambda j: back_copy(j, size).wait_recv())
    grads = ((kg_ref, key_ref), (vg_ref, value_ref))
    for n, (own_ref, _) in enumerate(grads):
        own_ref[rows - TAIL :] += after_ref[n].astype(jnp.float32)
    each(me + 1, shards, lambda p: part_copy(p, p).wait_recv())
    sum_ref[...] = jnp.sum(got_ref[...].astype(jnp.float32), axis=0)
    for t in range(SLOT_DEV):
        index = BLOCK - 1 - lead + BLOCK * t

        @pl.when(index < rows)
        def _():
            at = pl.ds(pl.multiple_of(jnp.minimum(index, rows - 1) - 7, 8), 8)
            ends = lax.broadcasted_iota(jnp.int32, (8, HEAD_DIM), 0) == 7
            for n, (own_ref, _) in enumerate(grads):
                for h in range(HEADS):
                    c = slice(h * HEAD_DIM, (h + 1) * HEAD_DIM)
                    r = (n * SLOT_DEV + t) * HEADS + h
                    own_ref[at, c] += jnp.where(ends, sum_ref[r : r + 1, :], 0.0)
    for own_ref, final_ref in grads:
        final_ref[...] = own_ref[...].astype(jnp.bfloat16)

    for size, fits in ways:
        @pl.when((me < last) & fits(lead_next))
        def _():
            def sent(j):
                for i in range(2):
                    halo_copy(i, j, size).wait_send()
            each(0, steps, sent)

        @pl.when((me > 0) & fits(lead))
        def _():
            each(0, steps, lambda j: back_copy(j, size).wait_send())
    each(me + 1, shards, lambda p: slot_copy(p, me).wait_send())
    each(0, me, lambda p: part_copy(p, me).wait_send())


def attention(query_rows, key_rows, value_rows, out_grad, own_slots):
    rows, feats = query_rows.shape
    shards = lax.axis_size("seq")
    slots = shards * SLOT_DEV
    half = SLOT_DEV * HEADS
    columns = TAIL + rows + slots
    steps = feats // (HEADS_STEP * HEAD_DIM)
    vmem = pl.BlockSpec(memory_space=pltpu.VMEM)
    bf16, f32 = jnp.bfloat16, jnp.float32
    return pl.pallas_call(
        functools.partial(kernel, shards),
        in_specs=[pl.BlockSpec(memory_space=pltpu.HBM)] * 4 + [vmem],
        out_specs=[vmem] * 4,
        out_shape=[jax.ShapeDtypeStruct((rows, feats), bf16)] * 4,
        scratch_shapes=[
            pltpu.VMEM((rows, feats), bf16),
            pltpu.VMEM((rows, feats), bf16),
            pltpu.VMEM((rows, feats), bf16),
            pltpu.VMEM((rows, feats), bf16),
            pltpu.VMEM((rows, feats), f32),
            pltpu.VMEM((rows, feats), f32),
            pltpu.VMEM((2, TAIL, feats), bf16),
            pltpu.VMEM((2 * half, HEAD_DIM), f32),
            pltpu.VMEM((rows, columns), f32),
            pltpu.VMEM((2, TAIL, feats), bf16),
            pltpu.VMEM((2, TAIL, feats), bf16),
            pltpu.VMEM((shards, 2 * half, HEAD_DIM), bf16),
            pltpu.VMEM((shards, 2 * half, HEAD_DIM), bf16),
            pltpu.VMEM((shards, 2 * half, HEAD_DIM), bf16),
            pltpu.VMEM((shards * half, HEAD_DIM), f32),
            pltpu.VMEM((shards * half, HEAD_DIM), f32),
            pltpu.VMEM((shards * half, HEAD_DIM), f32),
            pltpu.VMEM((shards * half, HEAD_DIM), f32),
            pltpu.SemaphoreType.DMA((2, steps)),
            pltpu.SemaphoreType.DMA((2, steps)),
            pltpu.SemaphoreType.DMA((shards,)),
            pltpu.SemaphoreType.DMA((shards,)),
            pltpu.SemaphoreType.DMA((steps,)),
            pltpu.SemaphoreType.DMA((steps,)),
            pltpu.SemaphoreType.DMA((shards,)),
            pltpu.SemaphoreType.DMA((shards,)),
            pltpu.SemaphoreType.DMA((4,)),
        ],
        compiler_params=pltpu.CompilerParams(
            vmem_limit_bytes=51 * 1024 * 1024, collective_id=0, has_side_effects=True
        ),
        cost_estimate=pl.CostEstimate(
            flops=10 * rows * columns * feats,
            bytes_accessed=24 * rows * feats,
            transcendentals=HEADS * rows * columns,
        ),
    )(query_rows, key_rows, value_rows, out_grad, own_slots)


def body(query_rows, key_rows, value_rows, out_grad):
    rows, feats = query_rows.shape
    shard = lax.axis_index("seq")
    lead = (shard * rows + OFF) % BLOCK
    index = [BLOCK - 1 - lead + BLOCK * i for i in range(SLOT_DEV)]
    own_slots = jnp.stack([
        jnp.concatenate([
            jnp.where(i < rows, lax.dynamic_slice_in_dim(array, jnp.minimum(i, rows - 1), 1, 0), 0)
            for i in index
        ])
        for array in (key_rows, value_rows)
    ])
    return tuple(
        attention(query_rows, key_rows, value_rows, out_grad, own_slots.reshape(-1, HEAD_DIM))
    )


def solution(mesh):
    spec = P(("groups", "seq"), None)
    return jax.shard_map(
        body, mesh=mesh, in_specs=(spec,) * 4, out_specs=(spec,) * 4, check_vma=False
    )
```

```python
import functools
import math

import jax
import jax.numpy as jnp
from jax import lax
from jax.experimental import pallas as pl
from jax.experimental.pallas import tpu as pltpu
from jax.sharding import PartitionSpec as P

HEADS = 16
HEAD_DIM = 128
BLOCK = 128
OFF = 32
TAIL = 96
SLOT_DEV = 2
HEADS_STEP = 4
SCALE = 1.0 / math.sqrt(HEAD_DIM)
NEG = -1e30


def bias_of(shard, rows, slots):
    first = shard * rows
    shape = (rows, TAIL + rows)
    query = first + lax.broadcasted_iota(jnp.int32, shape, 0)
    pos = first - TAIL + lax.broadcasted_iota(jnp.int32, shape, 1)
    local = (pos >= 0) & (pos <= query) & ((pos + OFF) >> 7 == (query + OFF) >> 7)
    shape = (rows, slots)
    query = first + lax.broadcasted_iota(jnp.int32, shape, 0)
    slot = lax.broadcasted_iota(jnp.int32, shape, 1)
    start = (slot >> 1) * rows
    offset = BLOCK - 1 - ((start + OFF) & (BLOCK - 1)) + BLOCK * (slot & 1)
    summary = (offset < rows) & ((start + offset + OFF) >> 7 < (query + OFF) >> 7)
    return (
        jnp.where(local, 0.0, NEG).astype(jnp.float32),
        jnp.where(summary, 0.0, NEG).astype(jnp.float32),
    )


def dot(a, b, dims):
    return lax.dot_general(a, b, (dims, ((), ())), preferred_element_type=jnp.float32)


NT = ((1,), (1,))
NN = ((1,), (0,))
TN = ((0,), (0,))


def one_head(q, k, v, g, bias):
    scores = dot(q, k, NT) * SCALE + bias
    top = jnp.max(scores, axis=1, keepdims=True)
    expo = jnp.exp(scores - top)
    prob = expo * (1.0 / jnp.sum(expo, axis=1, keepdims=True))
    weights = prob.astype(jnp.bfloat16)
    attended = dot(weights, v, NN).astype(jnp.bfloat16)
    delta = jnp.sum(g.astype(jnp.float32) * attended.astype(jnp.float32), axis=1, keepdims=True)
    dscores = (prob * (dot(g, v, NT) - delta)).astype(jnp.bfloat16)
    qgrad = (dot(dscores, k, NN) * SCALE).astype(jnp.bfloat16)
    return attended, qgrad, dot(dscores, q, TN) * SCALE, dot(weights, g, TN)


def remote(src, dst, send, recv, seq):
    return pltpu.make_async_remote_copy(
        src_ref=src, dst_ref=dst, send_sem=send, recv_sem=recv,
        device_id={"seq": seq}, device_id_type=pl.DeviceIdType.MESH,
    )


def kernel(shards, q_in, k_in, v_in, g_in, mine_ref, out_ref, qg_ref, key_ref, value_ref,
           q_ref, k_ref, v_ref, g_ref, kg_ref, vg_ref, after_ref, sum_ref, early_ref, late_ref, halo_ref, hg_ref, slot_ref, part_ref, got_ref, ks_ref, vs_ref,
           kp_ref, vp_ref, halo_send, halo_recv, slot_send, slot_recv, back_send, back_recv,
           part_send, part_recv, load_sem):
    rows, feats = q_ref.shape
    slots = shards * SLOT_DEV
    half = SLOT_DEV * HEADS
    wide = HEADS_STEP * HEAD_DIM
    steps = feats // wide
    me = lax.axis_index("seq")
    last = shards - 1
    prior, following = jnp.maximum(me - 1, 0), jnp.minimum(me + 1, last)
    lead = lax.rem(me * rows + OFF, BLOCK)
    lead_next = lax.rem((me + 1) * rows + OFF, BLOCK)
    ways = ((TAIL, lambda x: x > OFF), (OFF, lambda x: x <= OFF))

    loads = [
        pltpu.make_async_copy(source, target, load_sem.at[i])
        for i, (source, target) in enumerate(
            ((q_in, q_ref), (k_in, k_ref), (v_in, v_ref), (g_in, g_ref))
        )
    ]
    for load in loads:
        load.start()

    slot_ref[...] = jnp.zeros_like(slot_ref)
    got_ref[...] = jnp.zeros_like(got_ref)
    short = jnp.zeros((2, TAIL - OFF, feats), jnp.bfloat16)
    rest = jnp.zeros((2, OFF, feats), jnp.bfloat16)
    for ref, missing, alone in ((halo_ref, lead <= OFF, me == 0), (after_ref, lead_next <= OFF, me == last)):
        @pl.when(missing | alone)
        def _():
            ref[:, : TAIL - OFF] = short

        @pl.when(alone)
        def _():
            ref[:, TAIL - OFF :] = rest
    slot_ref[me] = mine_ref[...]

    barrier = pltpu.get_barrier_semaphore()

    def greet(p, carry):
        @pl.when(p != me)
        def _():
            pl.semaphore_signal(
                barrier, inc=1, device_id={"seq": p}, device_id_type=pl.DeviceIdType.MESH
            )
        return carry

    lax.fori_loop(0, shards, greet, 0)
    pl.semaphore_wait(barrier, shards - 1)

    def halo_copy(i, j, size):
        cols = pl.ds(pl.multiple_of(j * wide, wide), wide)
        return remote(
            (k_in, v_in)[i].at[pl.ds(rows - size, size), cols],
            halo_ref.at[i, pl.ds(TAIL - size, size), cols],
            halo_send.at[i, j], halo_recv.at[i, j], following,
        )

    def back_copy(j, size):
        part = (slice(None), pl.ds(TAIL - size, size), pl.ds(pl.multiple_of(j * wide, wide), wide))
        return remote(
            hg_ref.at[part], after_ref.at[part], back_send.at[j], back_recv.at[j], prior
        )

    def slot_copy(p, owner):
        return remote(mine_ref, slot_ref.at[owner], slot_send.at[p], slot_recv.at[owner], p)

    def part_copy(p, sender):
        return remote(part_ref.at[p], got_ref.at[sender], part_send.at[p], part_recv.at[sender], p)

    def each(low, high, action):
        def step(p, carry):
            action(p)
            return carry
        lax.fori_loop(low, high, step, 0)

    each(me + 1, shards, lambda p: slot_copy(p, me).start())
    for size, fits in ways:
        @pl.when((me < last) & fits(lead_next))
        def _():
            def send(j):
                for i in range(2):
                    halo_copy(i, j, size).start()
            each(0, steps, send)

    local, summary = bias_of(me, rows, slots)
    early_ref[:, : 2 * TAIL] = local[:TAIL, : 2 * TAIL]
    early_ref[:, 2 * TAIL :] = summary[:TAIL]
    late_ref[:, : rows - OFF] = local[TAIL:, TAIL + OFF :]
    late_ref[:, rows - OFF :] = summary[TAIL:]

    each(0, me, lambda p: slot_copy(p, p).wait_recv())

    ks_ref[...] = slot_ref[:, :half].astype(jnp.float32).reshape(shards * half, HEAD_DIM)
    vs_ref[...] = slot_ref[:, half:].astype(jnp.float32).reshape(shards * half, HEAD_DIM)

    for load in loads:
        load.wait()

    def group(j, carry):
        for size, fits in ways:
            @pl.when((me > 0) & fits(lead))
            def _():
                for i in range(2):
                    halo_copy(i, j, size).wait_recv()
        for i in range(HEADS_STEP):
            h = j * HEADS_STEP + i
            c = pl.ds(pl.multiple_of(h * HEAD_DIM, HEAD_DIM), HEAD_DIM)
            of_head = pl.ds(h, slots, stride=HEADS)
            k_slots = ks_ref[of_head, :].astype(jnp.bfloat16)
            v_slots = vs_ref[of_head, :].astype(jnp.bfloat16)
            k = jnp.concatenate([halo_ref[0, :, c], k_ref[:TAIL, c], k_slots], axis=0)
            v = jnp.concatenate([halo_ref[1, :, c], v_ref[:TAIL, c], v_slots], axis=0)
            out_ref[:TAIL, c], qg_ref[:TAIL, c], *early = one_head(
                q_ref[:TAIL, c], k, v, g_ref[:TAIL, c], early_ref[...]
            )
            k = jnp.concatenate([k_ref[OFF:, c], k_slots], axis=0)
            v = jnp.concatenate([v_ref[OFF:, c], v_slots], axis=0)
            out_ref[TAIL:, c], qg_ref[TAIL:, c], *late = one_head(
                q_ref[TAIL:, c], k, v, g_ref[TAIL:, c], late_ref[...]
            )
            for n, (own_ref, term_ref) in enumerate(((kg_ref, kp_ref), (vg_ref, vp_ref))):
                hg_ref[n, :, c] = early[n][:TAIL].astype(jnp.bfloat16)
                own_ref[:OFF, c] = early[n][TAIL : TAIL + OFF]
                own_ref[OFF:TAIL, c] = early[n][TAIL + OFF : 2 * TAIL] + late[n][: TAIL - OFF]
                own_ref[TAIL:, c] = late[n][TAIL - OFF : rows - OFF]
                term_ref[of_head, :] = early[n][2 * TAIL :] + late[n][rows - OFF :]
        for size, fits in ways:
            @pl.when((me > 0) & fits(lead))
            def _():
                back_copy(j, size).start()
        return carry

    lax.fori_loop(0, steps, group, 0)

    part_ref[:, :half] = kp_ref[...].astype(jnp.bfloat16).reshape(shards, half, HEAD_DIM)
    part_ref[:, half:] = vp_ref[...].astype(jnp.bfloat16).reshape(shards, half, HEAD_DIM)
    each(0, me, lambda p: part_copy(p, me).start())
    got_ref[me] = part_ref[me]
    for size, fits in ways:
        @pl.when((me < last) & fits(lead_next))
        def _():
            each(0, steps, lambda j: back_copy(j, size).wait_recv())
    grads = ((kg_ref, key_ref), (vg_ref, value_ref))
    for n, (own_ref, _) in enumerate(grads):
        own_ref[rows - TAIL :] += after_ref[n].astype(jnp.float32)
    each(me + 1, shards, lambda p: part_copy(p, p).wait_recv())
    sum_ref[...] = jnp.sum(got_ref[...].astype(jnp.float32), axis=0)
    for t in range(SLOT_DEV):
        index = BLOCK - 1 - lead + BLOCK * t

        @pl.when(index < rows)
        def _():
            at = pl.ds(pl.multiple_of(jnp.minimum(index, rows - 1) - 7, 8), 8)
            ends = lax.broadcasted_iota(jnp.int32, (8, HEAD_DIM), 0) == 7
            for n, (own_ref, _) in enumerate(grads):
                for h in range(HEADS):
                    c = slice(h * HEAD_DIM, (h + 1) * HEAD_DIM)
                    r = (n * SLOT_DEV + t) * HEADS + h
                    own_ref[at, c] += jnp.where(ends, sum_ref[r : r + 1, :], 0.0)
    for own_ref, final_ref in grads:
        final_ref[...] = own_ref[...].astype(jnp.bfloat16)

    for size, fits in ways:
        @pl.when((me < last) & fits(lead_next))
        def _():
            def sent(j):
                for i in range(2):
                    halo_copy(i, j, size).wait_send()
            each(0, steps, sent)

        @pl.when((me > 0) & fits(lead))
        def _():
            each(0, steps, lambda j: back_copy(j, size).wait_send())
    each(me + 1, shards, lambda p: slot_copy(p, me).wait_send())
    each(0, me, lambda p: part_copy(p, me).wait_send())


def attention(query_rows, key_rows, value_rows, out_grad, own_slots):
    rows, feats = query_rows.shape
    shards = lax.axis_size("seq")
    slots = shards * SLOT_DEV
    half = SLOT_DEV * HEADS
    columns = TAIL + rows + slots
    steps = feats // (HEADS_STEP * HEAD_DIM)
    vmem = pl.BlockSpec(memory_space=pltpu.VMEM)
    bf16, f32 = jnp.bfloat16, jnp.float32
    return pl.pallas_call(
        functools.partial(kernel, shards),
        in_specs=[pl.BlockSpec(memory_space=pltpu.HBM)] * 4 + [vmem],
        out_specs=[vmem] * 4,
        out_shape=[jax.ShapeDtypeStruct((rows, feats), bf16)] * 4,
        scratch_shapes=[
            pltpu.VMEM((rows, feats), bf16),
            pltpu.VMEM((rows, feats), bf16),
            pltpu.VMEM((rows, feats), bf16),
            pltpu.VMEM((rows, feats), bf16),
            pltpu.VMEM((rows, feats), f32),
            pltpu.VMEM((rows, feats), f32),
            pltpu.VMEM((2, TAIL, feats), bf16),
            pltpu.VMEM((2 * half, HEAD_DIM), f32),
            pltpu.VMEM((TAIL, 2 * TAIL + slots), f32),
            pltpu.VMEM((rows - TAIL, rows - OFF + slots), f32),
            pltpu.VMEM((2, TAIL, feats), bf16),
            pltpu.VMEM((2, TAIL, feats), bf16),
            pltpu.VMEM((shards, 2 * half, HEAD_DIM), bf16),
            pltpu.VMEM((shards, 2 * half, HEAD_DIM), bf16),
            pltpu.VMEM((shards, 2 * half, HEAD_DIM), bf16),
            pltpu.VMEM((shards * half, HEAD_DIM), f32),
            pltpu.VMEM((shards * half, HEAD_DIM), f32),
            pltpu.VMEM((shards * half, HEAD_DIM), f32),
            pltpu.VMEM((shards * half, HEAD_DIM), f32),
            pltpu.SemaphoreType.DMA((2, steps)),
            pltpu.SemaphoreType.DMA((2, steps)),
            pltpu.SemaphoreType.DMA((shards,)),
            pltpu.SemaphoreType.DMA((shards,)),
            pltpu.SemaphoreType.DMA((steps,)),
            pltpu.SemaphoreType.DMA((steps,)),
            pltpu.SemaphoreType.DMA((shards,)),
            pltpu.SemaphoreType.DMA((shards,)),
            pltpu.SemaphoreType.DMA((4,)),
        ],
        compiler_params=pltpu.CompilerParams(
            vmem_limit_bytes=51 * 1024 * 1024, collective_id=0, has_side_effects=True
        ),
        cost_estimate=pl.CostEstimate(
            flops=10 * rows * columns * feats,
            bytes_accessed=24 * rows * feats,
            transcendentals=HEADS * rows * columns,
        ),
    )(query_rows, key_rows, value_rows, out_grad, own_slots)


def body(query_rows, key_rows, value_rows, out_grad):
    rows, feats = query_rows.shape
    shard = lax.axis_index("seq")
    lead = (shard * rows + OFF) % BLOCK
    index = [BLOCK - 1 - lead + BLOCK * i for i in range(SLOT_DEV)]
    own_slots = jnp.stack([
        jnp.concatenate([
            jnp.where(i < rows, lax.dynamic_slice_in_dim(array, jnp.minimum(i, rows - 1), 1, 0), 0)
            for i in index
        ])
        for array in (key_rows, value_rows)
    ])
    return tuple(
        attention(query_rows, key_rows, value_rows, out_grad, own_slots.reshape(-1, HEAD_DIM))
    )


def solution(mesh):
    spec = P(("groups", "seq"), None)
    return jax.shard_map(
        body, mesh=mesh, in_specs=(spec,) * 4, out_specs=(spec,) * 4, check_vma=False
    )
```

```python
import functools
import math

import jax
import jax.numpy as jnp
from jax import lax
from jax.experimental import pallas as pl
from jax.experimental.pallas import tpu as pltpu
from jax.sharding import PartitionSpec as P

HEADS = 16
HEAD_DIM = 128
BLOCK = 128
OFF = 32
TAIL = 96
SLOT_DEV = 2
HEADS_STEP = 4
SCALE = 1.0 / math.sqrt(HEAD_DIM)
NEG = -1e30


def bias_of(shard, rows, slots):
    first = shard * rows
    shape = (rows, TAIL + rows)
    query = first + lax.broadcasted_iota(jnp.int32, shape, 0)
    pos = first - TAIL + lax.broadcasted_iota(jnp.int32, shape, 1)
    local = (pos >= 0) & (pos <= query) & ((pos + OFF) >> 7 == (query + OFF) >> 7)
    shape = (rows, slots)
    query = first + lax.broadcasted_iota(jnp.int32, shape, 0)
    slot = lax.broadcasted_iota(jnp.int32, shape, 1)
    start = (slot >> 1) * rows
    offset = BLOCK - 1 - ((start + OFF) & (BLOCK - 1)) + BLOCK * (slot & 1)
    summary = (offset < rows) & ((start + offset + OFF) >> 7 < (query + OFF) >> 7)
    return (
        jnp.where(local, 0.0, NEG).astype(jnp.float32),
        jnp.where(summary, 0.0, NEG).astype(jnp.float32),
    )


def dot(a, b, dims):
    return lax.dot_general(a, b, (dims, ((), ())), preferred_element_type=jnp.float32)


NT = ((1,), (1,))
NN = ((1,), (0,))
TN = ((0,), (0,))


def all_chains(chains):
    scores = [dot(q, k, NT) * SCALE + bias for q, k, v, g, bias in chains]
    dweights = [dot(g, v, NT) for q, k, v, g, bias in chains]
    tops = [jnp.max(x, axis=1, keepdims=True) for x in scores]
    expos = [jnp.exp(x - top) for x, top in zip(scores, tops)]
    totals = [jnp.sum(x, axis=1, keepdims=True) for x in expos]
    probs = [x * (1.0 / total) for x, total in zip(expos, totals)]
    weights = [x.astype(jnp.bfloat16) for x in probs]
    attended = [dot(w, c[2], NN).astype(jnp.bfloat16) for w, c in zip(weights, chains)]
    vgrads = [dot(w, c[3], TN) for w, c in zip(weights, chains)]
    deltas = [
        jnp.sum(c[3].astype(jnp.float32) * x.astype(jnp.float32), axis=1, keepdims=True)
        for x, c in zip(attended, chains)
    ]
    dscores = [
        (p * (dw - delta)).astype(jnp.bfloat16) for p, dw, delta in zip(probs, dweights, deltas)
    ]
    qgrads = [(dot(ds, c[1], NN) * SCALE).astype(jnp.bfloat16) for ds, c in zip(dscores, chains)]
    kgrads = [dot(ds, c[0], TN) * SCALE for ds, c in zip(dscores, chains)]
    return list(zip(attended, qgrads, kgrads, vgrads))


def remote(src, dst, send, recv, seq):
    return pltpu.make_async_remote_copy(
        src_ref=src, dst_ref=dst, send_sem=send, recv_sem=recv,
        device_id={"seq": seq}, device_id_type=pl.DeviceIdType.MESH,
    )


def kernel(shards, q_in, k_in, v_in, g_in, mine_ref, out_ref, qg_ref, key_ref, value_ref,
           q_ref, k_ref, v_ref, g_ref, kg_ref, vg_ref, after_ref, sum_ref, early_ref, late_ref, halo_ref, hg_ref, slot_ref, part_ref, got_ref, ks_ref, vs_ref,
           kp_ref, vp_ref, halo_send, halo_recv, slot_send, slot_recv, back_send, back_recv,
           part_send, part_recv, load_sem):
    rows, feats = q_ref.shape
    slots = shards * SLOT_DEV
    half = SLOT_DEV * HEADS
    wide = HEADS_STEP * HEAD_DIM
    steps = feats // wide
    me = lax.axis_index("seq")
    last = shards - 1
    prior, following = jnp.maximum(me - 1, 0), jnp.minimum(me + 1, last)
    lead = lax.rem(me * rows + OFF, BLOCK)
    lead_next = lax.rem((me + 1) * rows + OFF, BLOCK)
    ways = ((TAIL, lambda x: x > OFF), (OFF, lambda x: x <= OFF))

    loads = [
        pltpu.make_async_copy(source, target, load_sem.at[i])
        for i, (source, target) in enumerate(
            ((q_in, q_ref), (k_in, k_ref), (v_in, v_ref), (g_in, g_ref))
        )
    ]
    for load in loads:
        load.start()

    slot_ref[...] = jnp.zeros_like(slot_ref)
    got_ref[...] = jnp.zeros_like(got_ref)
    short = jnp.zeros((2, TAIL - OFF, feats), jnp.bfloat16)
    rest = jnp.zeros((2, OFF, feats), jnp.bfloat16)
    for ref, missing, alone in ((halo_ref, lead <= OFF, me == 0), (after_ref, lead_next <= OFF, me == last)):
        @pl.when(missing | alone)
        def _():
            ref[:, : TAIL - OFF] = short

        @pl.when(alone)
        def _():
            ref[:, TAIL - OFF :] = rest
    slot_ref[me] = mine_ref[...]

    barrier = pltpu.get_barrier_semaphore()

    def greet(p, carry):
        @pl.when(p != me)
        def _():
            pl.semaphore_signal(
                barrier, inc=1, device_id={"seq": p}, device_id_type=pl.DeviceIdType.MESH
            )
        return carry

    lax.fori_loop(0, shards, greet, 0)
    pl.semaphore_wait(barrier, shards - 1)

    def halo_copy(i, j, size):
        cols = pl.ds(pl.multiple_of(j * wide, wide), wide)
        return remote(
            (k_in, v_in)[i].at[pl.ds(rows - size, size), cols],
            halo_ref.at[i, pl.ds(TAIL - size, size), cols],
            halo_send.at[i, j], halo_recv.at[i, j], following,
        )

    def back_copy(j, size):
        part = (slice(None), pl.ds(TAIL - size, size), pl.ds(pl.multiple_of(j * wide, wide), wide))
        return remote(
            hg_ref.at[part], after_ref.at[part], back_send.at[j], back_recv.at[j], prior
        )

    def slot_copy(p, owner):
        return remote(mine_ref, slot_ref.at[owner], slot_send.at[p], slot_recv.at[owner], p)

    def part_copy(p, sender):
        return remote(part_ref.at[p], got_ref.at[sender], part_send.at[p], part_recv.at[sender], p)

    def each(low, high, action):
        def step(p, carry):
            action(p)
            return carry
        lax.fori_loop(low, high, step, 0)

    each(me + 1, shards, lambda p: slot_copy(p, me).start())
    for size, fits in ways:
        @pl.when((me < last) & fits(lead_next))
        def _():
            def send(j):
                for i in range(2):
                    halo_copy(i, j, size).start()
            each(0, steps, send)

    local, summary = bias_of(me, rows, slots)
    early_ref[:, : 2 * TAIL] = local[:TAIL, : 2 * TAIL]
    early_ref[:, 2 * TAIL :] = summary[:TAIL]
    late_ref[:, : rows - OFF] = local[TAIL:, TAIL + OFF :]
    late_ref[:, rows - OFF :] = summary[TAIL:]

    each(0, me, lambda p: slot_copy(p, p).wait_recv())

    ks_ref[...] = slot_ref[:, :half].astype(jnp.float32).reshape(shards * half, HEAD_DIM)
    vs_ref[...] = slot_ref[:, half:].astype(jnp.float32).reshape(shards * half, HEAD_DIM)

    for load in loads:
        load.wait()

    def group(j, carry):
        for size, fits in ways:
            @pl.when((me > 0) & fits(lead))
            def _():
                for i in range(2):
                    halo_copy(i, j, size).wait_recv()
        chains = []
        places = []
        for i in range(HEADS_STEP):
            h = j * HEADS_STEP + i
            c = pl.ds(pl.multiple_of(h * HEAD_DIM, HEAD_DIM), HEAD_DIM)
            of_head = pl.ds(h, slots, stride=HEADS)
            places.append((c, of_head))
            k_slots = ks_ref[of_head, :].astype(jnp.bfloat16)
            v_slots = vs_ref[of_head, :].astype(jnp.bfloat16)
            k = jnp.concatenate([halo_ref[0, :, c], k_ref[:TAIL, c], k_slots], axis=0)
            v = jnp.concatenate([halo_ref[1, :, c], v_ref[:TAIL, c], v_slots], axis=0)
            chains.append((q_ref[:TAIL, c], k, v, g_ref[:TAIL, c], early_ref[...]))
            k = jnp.concatenate([k_ref[OFF:, c], k_slots], axis=0)
            v = jnp.concatenate([v_ref[OFF:, c], v_slots], axis=0)
            chains.append((q_ref[TAIL:, c], k, v, g_ref[TAIL:, c], late_ref[...]))
        results = all_chains(chains)
        for i, (c, of_head) in enumerate(places):
            out_ref[:TAIL, c], qg_ref[:TAIL, c], *early = results[2 * i]
            out_ref[TAIL:, c], qg_ref[TAIL:, c], *late = results[2 * i + 1]
            for n, (own_ref, term_ref) in enumerate(((kg_ref, kp_ref), (vg_ref, vp_ref))):
                hg_ref[n, :, c] = early[n][:TAIL].astype(jnp.bfloat16)
                own_ref[:OFF, c] = early[n][TAIL : TAIL + OFF]
                own_ref[OFF:TAIL, c] = early[n][TAIL + OFF : 2 * TAIL] + late[n][: TAIL - OFF]
                own_ref[TAIL:, c] = late[n][TAIL - OFF : rows - OFF]
                term_ref[of_head, :] = early[n][2 * TAIL :] + late[n][rows - OFF :]
        for size, fits in ways:
            @pl.when((me > 0) & fits(lead))
            def _():
                back_copy(j, size).start()
        return carry

    lax.fori_loop(0, steps, group, 0)

    part_ref[:, :half] = kp_ref[...].astype(jnp.bfloat16).reshape(shards, half, HEAD_DIM)
    part_ref[:, half:] = vp_ref[...].astype(jnp.bfloat16).reshape(shards, half, HEAD_DIM)
    each(0, me, lambda p: part_copy(p, me).start())
    got_ref[me] = part_ref[me]
    for size, fits in ways:
        @pl.when((me < last) & fits(lead_next))
        def _():
            each(0, steps, lambda j: back_copy(j, size).wait_recv())
    grads = ((kg_ref, key_ref), (vg_ref, value_ref))
    for n, (own_ref, _) in enumerate(grads):
        own_ref[rows - TAIL :] += after_ref[n].astype(jnp.float32)
    each(me + 1, shards, lambda p: part_copy(p, p).wait_recv())
    sum_ref[...] = jnp.sum(got_ref[...].astype(jnp.float32), axis=0)
    for t in range(SLOT_DEV):
        index = BLOCK - 1 - lead + BLOCK * t

        @pl.when(index < rows)
        def _():
            at = pl.ds(pl.multiple_of(jnp.minimum(index, rows - 1) - 7, 8), 8)
            ends = lax.broadcasted_iota(jnp.int32, (8, HEAD_DIM), 0) == 7
            for n, (own_ref, _) in enumerate(grads):
                for h in range(HEADS):
                    c = slice(h * HEAD_DIM, (h + 1) * HEAD_DIM)
                    r = (n * SLOT_DEV + t) * HEADS + h
                    own_ref[at, c] += jnp.where(ends, sum_ref[r : r + 1, :], 0.0)
    for own_ref, final_ref in grads:
        final_ref[...] = own_ref[...].astype(jnp.bfloat16)

    for size, fits in ways:
        @pl.when((me < last) & fits(lead_next))
        def _():
            def sent(j):
                for i in range(2):
                    halo_copy(i, j, size).wait_send()
            each(0, steps, sent)

        @pl.when((me > 0) & fits(lead))
        def _():
            each(0, steps, lambda j: back_copy(j, size).wait_send())
    each(me + 1, shards, lambda p: slot_copy(p, me).wait_send())
    each(0, me, lambda p: part_copy(p, me).wait_send())


def attention(query_rows, key_rows, value_rows, out_grad, own_slots):
    rows, feats = query_rows.shape
    shards = lax.axis_size("seq")
    slots = shards * SLOT_DEV
    half = SLOT_DEV * HEADS
    columns = TAIL + rows + slots
    steps = feats // (HEADS_STEP * HEAD_DIM)
    vmem = pl.BlockSpec(memory_space=pltpu.VMEM)
    bf16, f32 = jnp.bfloat16, jnp.float32
    return pl.pallas_call(
        functools.partial(kernel, shards),
        in_specs=[pl.BlockSpec(memory_space=pltpu.HBM)] * 4 + [vmem],
        out_specs=[vmem] * 4,
        out_shape=[jax.ShapeDtypeStruct((rows, feats), bf16)] * 4,
        scratch_shapes=[
            pltpu.VMEM((rows, feats), bf16),
            pltpu.VMEM((rows, feats), bf16),
            pltpu.VMEM((rows, feats), bf16),
            pltpu.VMEM((rows, feats), bf16),
            pltpu.VMEM((rows, feats), f32),
            pltpu.VMEM((rows, feats), f32),
            pltpu.VMEM((2, TAIL, feats), bf16),
            pltpu.VMEM((2 * half, HEAD_DIM), f32),
            pltpu.VMEM((TAIL, 2 * TAIL + slots), f32),
            pltpu.VMEM((rows - TAIL, rows - OFF + slots), f32),
            pltpu.VMEM((2, TAIL, feats), bf16),
            pltpu.VMEM((2, TAIL, feats), bf16),
            pltpu.VMEM((shards, 2 * half, HEAD_DIM), bf16),
            pltpu.VMEM((shards, 2 * half, HEAD_DIM), bf16),
            pltpu.VMEM((shards, 2 * half, HEAD_DIM), bf16),
            pltpu.VMEM((shards * half, HEAD_DIM), f32),
            pltpu.VMEM((shards * half, HEAD_DIM), f32),
            pltpu.VMEM((shards * half, HEAD_DIM), f32),
            pltpu.VMEM((shards * half, HEAD_DIM), f32),
            pltpu.SemaphoreType.DMA((2, steps)),
            pltpu.SemaphoreType.DMA((2, steps)),
            pltpu.SemaphoreType.DMA((shards,)),
            pltpu.SemaphoreType.DMA((shards,)),
            pltpu.SemaphoreType.DMA((steps,)),
            pltpu.SemaphoreType.DMA((steps,)),
            pltpu.SemaphoreType.DMA((shards,)),
            pltpu.SemaphoreType.DMA((shards,)),
            pltpu.SemaphoreType.DMA((4,)),
        ],
        compiler_params=pltpu.CompilerParams(
            vmem_limit_bytes=51 * 1024 * 1024, collective_id=0, has_side_effects=True
        ),
        cost_estimate=pl.CostEstimate(
            flops=10 * rows * columns * feats,
            bytes_accessed=24 * rows * feats,
            transcendentals=HEADS * rows * columns,
        ),
    )(query_rows, key_rows, value_rows, out_grad, own_slots)


def body(query_rows, key_rows, value_rows, out_grad):
    rows, feats = query_rows.shape
    shard = lax.axis_index("seq")
    lead = (shard * rows + OFF) % BLOCK
    index = [BLOCK - 1 - lead + BLOCK * i for i in range(SLOT_DEV)]
    own_slots = jnp.stack([
        jnp.concatenate([
            jnp.where(i < rows, lax.dynamic_slice_in_dim(array, jnp.minimum(i, rows - 1), 1, 0), 0)
            for i in index
        ])
        for array in (key_rows, value_rows)
    ])
    return tuple(
        attention(query_rows, key_rows, value_rows, out_grad, own_slots.reshape(-1, HEAD_DIM))
    )


def solution(mesh):
    spec = P(("groups", "seq"), None)
    return jax.shard_map(
        body, mesh=mesh, in_specs=(spec,) * 4, out_specs=(spec,) * 4, check_vma=False
    )
```

```python
import functools
import math

import jax
import jax.numpy as jnp
from jax import lax
from jax.experimental import pallas as pl
from jax.experimental.pallas import tpu as pltpu
from jax.sharding import PartitionSpec as P

HEADS = 16
HEAD_DIM = 128
BLOCK = 128
OFF = 32
TAIL = 96
SLOT_DEV = 2
HEADS_STEP = 8
SCALE = 1.0 / math.sqrt(HEAD_DIM)
NEG = -1e30


def bias_of(shard, rows, slots):
    first = shard * rows
    shape = (rows, TAIL + rows)
    query = first + lax.broadcasted_iota(jnp.int32, shape, 0)
    pos = first - TAIL + lax.broadcasted_iota(jnp.int32, shape, 1)
    local = (pos >= 0) & (pos <= query) & ((pos + OFF) >> 7 == (query + OFF) >> 7)
    shape = (rows, slots)
    query = first + lax.broadcasted_iota(jnp.int32, shape, 0)
    slot = lax.broadcasted_iota(jnp.int32, shape, 1)
    start = (slot >> 1) * rows
    offset = BLOCK - 1 - ((start + OFF) & (BLOCK - 1)) + BLOCK * (slot & 1)
    summary = (offset < rows) & ((start + offset + OFF) >> 7 < (query + OFF) >> 7)
    return (
        jnp.where(local, 0.0, NEG).astype(jnp.float32),
        jnp.where(summary, 0.0, NEG).astype(jnp.float32),
    )


def dot(a, b, dims):
    return lax.dot_general(a, b, (dims, ((), ())), preferred_element_type=jnp.float32)


NT = ((1,), (1,))
NN = ((1,), (0,))
TN = ((0,), (0,))


def all_chains(chains):
    scores = [dot(q, k, NT) * SCALE + bias for q, k, v, g, bias in chains]
    dweights = [dot(g, v, NT) for q, k, v, g, bias in chains]
    tops = [jnp.max(x, axis=1, keepdims=True) for x in scores]
    expos = [jnp.exp(x - top) for x, top in zip(scores, tops)]
    totals = [jnp.sum(x, axis=1, keepdims=True) for x in expos]
    probs = [x * (1.0 / total) for x, total in zip(expos, totals)]
    weights = [x.astype(jnp.bfloat16) for x in probs]
    attended = [dot(w, c[2], NN).astype(jnp.bfloat16) for w, c in zip(weights, chains)]
    vgrads = [dot(w, c[3], TN) for w, c in zip(weights, chains)]
    deltas = [
        jnp.sum(c[3].astype(jnp.float32) * x.astype(jnp.float32), axis=1, keepdims=True)
        for x, c in zip(attended, chains)
    ]
    dscores = [
        (p * (dw - delta)).astype(jnp.bfloat16) for p, dw, delta in zip(probs, dweights, deltas)
    ]
    qgrads = [(dot(ds, c[1], NN) * SCALE).astype(jnp.bfloat16) for ds, c in zip(dscores, chains)]
    kgrads = [dot(ds, c[0], TN) * SCALE for ds, c in zip(dscores, chains)]
    return list(zip(attended, qgrads, kgrads, vgrads))


def remote(src, dst, send, recv, seq):
    return pltpu.make_async_remote_copy(
        src_ref=src, dst_ref=dst, send_sem=send, recv_sem=recv,
        device_id={"seq": seq}, device_id_type=pl.DeviceIdType.MESH,
    )


def kernel(shards, q_in, k_in, v_in, g_in, mine_ref, out_ref, qg_ref, key_ref, value_ref,
           q_ref, k_ref, v_ref, g_ref, kg_ref, vg_ref, after_ref, sum_ref, early_ref, late_ref, halo_ref, hg_ref, slot_ref, part_ref, got_ref, ks_ref, vs_ref,
           kp_ref, vp_ref, halo_send, halo_recv, slot_send, slot_recv, back_send, back_recv,
           part_send, part_recv, load_sem):
    rows, feats = q_ref.shape
    slots = shards * SLOT_DEV
    half = SLOT_DEV * HEADS
    wide = HEADS_STEP * HEAD_DIM
    steps = feats // wide
    me = lax.axis_index("seq")
    last = shards - 1
    prior, following = jnp.maximum(me - 1, 0), jnp.minimum(me + 1, last)
    lead = lax.rem(me * rows + OFF, BLOCK)
    lead_next = lax.rem((me + 1) * rows + OFF, BLOCK)
    ways = ((TAIL, lambda x: x > OFF), (OFF, lambda x: x <= OFF))

    loads = [
        pltpu.make_async_copy(source, target, load_sem.at[i])
        for i, (source, target) in enumerate(
            ((q_in, q_ref), (k_in, k_ref), (v_in, v_ref), (g_in, g_ref))
        )
    ]
    for load in loads:
        load.start()

    slot_ref[...] = jnp.zeros_like(slot_ref)
    got_ref[...] = jnp.zeros_like(got_ref)
    short = jnp.zeros((2, TAIL - OFF, feats), jnp.bfloat16)
    rest = jnp.zeros((2, OFF, feats), jnp.bfloat16)
    for ref, missing, alone in ((halo_ref, lead <= OFF, me == 0), (after_ref, lead_next <= OFF, me == last)):
        @pl.when(missing | alone)
        def _():
            ref[:, : TAIL - OFF] = short

        @pl.when(alone)
        def _():
            ref[:, TAIL - OFF :] = rest
    slot_ref[me] = mine_ref[...]

    barrier = pltpu.get_barrier_semaphore()

    def greet(p, carry):
        @pl.when(p != me)
        def _():
            pl.semaphore_signal(
                barrier, inc=1, device_id={"seq": p}, device_id_type=pl.DeviceIdType.MESH
            )
        return carry

    lax.fori_loop(0, shards, greet, 0)
    pl.semaphore_wait(barrier, shards - 1)

    def halo_copy(i, j, size):
        cols = pl.ds(pl.multiple_of(j * wide, wide), wide)
        return remote(
            (k_in, v_in)[i].at[pl.ds(rows - size, size), cols],
            halo_ref.at[i, pl.ds(TAIL - size, size), cols],
            halo_send.at[i, j], halo_recv.at[i, j], following,
        )

    def back_copy(j, size):
        part = (slice(None), pl.ds(TAIL - size, size), pl.ds(pl.multiple_of(j * wide, wide), wide))
        return remote(
            hg_ref.at[part], after_ref.at[part], back_send.at[j], back_recv.at[j], prior
        )

    def slot_copy(p, owner):
        return remote(mine_ref, slot_ref.at[owner], slot_send.at[p], slot_recv.at[owner], p)

    def part_copy(p, sender):
        return remote(part_ref.at[p], got_ref.at[sender], part_send.at[p], part_recv.at[sender], p)

    def each(low, high, action):
        def step(p, carry):
            action(p)
            return carry
        lax.fori_loop(low, high, step, 0)

    each(me + 1, shards, lambda p: slot_copy(p, me).start())
    for size, fits in ways:
        @pl.when((me < last) & fits(lead_next))
        def _():
            def send(j):
                for i in range(2):
                    halo_copy(i, j, size).start()
            each(0, steps, send)

    local, summary = bias_of(me, rows, slots)
    early_ref[:, : 2 * TAIL] = local[:TAIL, : 2 * TAIL]
    early_ref[:, 2 * TAIL :] = summary[:TAIL]
    late_ref[:, : rows - OFF] = local[TAIL:, TAIL + OFF :]
    late_ref[:, rows - OFF :] = summary[TAIL:]

    each(0, me, lambda p: slot_copy(p, p).wait_recv())

    ks_ref[...] = slot_ref[:, :half].astype(jnp.float32).reshape(shards * half, HEAD_DIM)
    vs_ref[...] = slot_ref[:, half:].astype(jnp.float32).reshape(shards * half, HEAD_DIM)

    for load in loads:
        load.wait()

    def group(j, carry):
        for size, fits in ways:
            @pl.when((me > 0) & fits(lead))
            def _():
                for i in range(2):
                    halo_copy(i, j, size).wait_recv()
        chains = []
        places = []
        for i in range(HEADS_STEP):
            h = j * HEADS_STEP + i
            c = pl.ds(pl.multiple_of(h * HEAD_DIM, HEAD_DIM), HEAD_DIM)
            of_head = pl.ds(h, slots, stride=HEADS)
            places.append((c, of_head))
            k_slots = ks_ref[of_head, :].astype(jnp.bfloat16)
            v_slots = vs_ref[of_head, :].astype(jnp.bfloat16)
            k = jnp.concatenate([halo_ref[0, :, c], k_ref[:TAIL, c], k_slots], axis=0)
            v = jnp.concatenate([halo_ref[1, :, c], v_ref[:TAIL, c], v_slots], axis=0)
            chains.append((q_ref[:TAIL, c], k, v, g_ref[:TAIL, c], early_ref[...]))
            k = jnp.concatenate([k_ref[OFF:, c], k_slots], axis=0)
            v = jnp.concatenate([v_ref[OFF:, c], v_slots], axis=0)
            chains.append((q_ref[TAIL:, c], k, v, g_ref[TAIL:, c], late_ref[...]))
        results = all_chains(chains)
        for i, (c, of_head) in enumerate(places):
            out_ref[:TAIL, c], qg_ref[:TAIL, c], *early = results[2 * i]
            out_ref[TAIL:, c], qg_ref[TAIL:, c], *late = results[2 * i + 1]
            for n, (own_ref, term_ref) in enumerate(((kg_ref, kp_ref), (vg_ref, vp_ref))):
                hg_ref[n, :, c] = early[n][:TAIL].astype(jnp.bfloat16)
                own_ref[:OFF, c] = early[n][TAIL : TAIL + OFF]
                own_ref[OFF:TAIL, c] = early[n][TAIL + OFF : 2 * TAIL] + late[n][: TAIL - OFF]
                own_ref[TAIL:, c] = late[n][TAIL - OFF : rows - OFF]
                term_ref[of_head, :] = early[n][2 * TAIL :] + late[n][rows - OFF :]
        for size, fits in ways:
            @pl.when((me > 0) & fits(lead))
            def _():
                back_copy(j, size).start()
        return carry

    lax.fori_loop(0, steps, group, 0)

    part_ref[:, :half] = kp_ref[...].astype(jnp.bfloat16).reshape(shards, half, HEAD_DIM)
    part_ref[:, half:] = vp_ref[...].astype(jnp.bfloat16).reshape(shards, half, HEAD_DIM)
    each(0, me, lambda p: part_copy(p, me).start())
    got_ref[me] = part_ref[me]
    for size, fits in ways:
        @pl.when((me < last) & fits(lead_next))
        def _():
            each(0, steps, lambda j: back_copy(j, size).wait_recv())
    grads = ((kg_ref, key_ref), (vg_ref, value_ref))
    for n, (own_ref, _) in enumerate(grads):
        own_ref[rows - TAIL :] += after_ref[n].astype(jnp.float32)
    each(me + 1, shards, lambda p: part_copy(p, p).wait_recv())
    sum_ref[...] = jnp.sum(got_ref[...].astype(jnp.float32), axis=0)
    for t in range(SLOT_DEV):
        index = BLOCK - 1 - lead + BLOCK * t

        @pl.when(index < rows)
        def _():
            at = pl.ds(pl.multiple_of(jnp.minimum(index, rows - 1) - 7, 8), 8)
            ends = lax.broadcasted_iota(jnp.int32, (8, HEAD_DIM), 0) == 7
            for n, (own_ref, _) in enumerate(grads):
                for h in range(HEADS):
                    c = slice(h * HEAD_DIM, (h + 1) * HEAD_DIM)
                    r = (n * SLOT_DEV + t) * HEADS + h
                    own_ref[at, c] += jnp.where(ends, sum_ref[r : r + 1, :], 0.0)
    for own_ref, final_ref in grads:
        final_ref[...] = own_ref[...].astype(jnp.bfloat16)

    for size, fits in ways:
        @pl.when((me < last) & fits(lead_next))
        def _():
            def sent(j):
                for i in range(2):
                    halo_copy(i, j, size).wait_send()
            each(0, steps, sent)

        @pl.when((me > 0) & fits(lead))
        def _():
            each(0, steps, lambda j: back_copy(j, size).wait_send())
    each(me + 1, shards, lambda p: slot_copy(p, me).wait_send())
    each(0, me, lambda p: part_copy(p, me).wait_send())


def attention(query_rows, key_rows, value_rows, out_grad, own_slots):
    rows, feats = query_rows.shape
    shards = lax.axis_size("seq")
    slots = shards * SLOT_DEV
    half = SLOT_DEV * HEADS
    columns = TAIL + rows + slots
    steps = feats // (HEADS_STEP * HEAD_DIM)
    vmem = pl.BlockSpec(memory_space=pltpu.VMEM)
    bf16, f32 = jnp.bfloat16, jnp.float32
    return pl.pallas_call(
        functools.partial(kernel, shards),
        in_specs=[pl.BlockSpec(memory_space=pltpu.HBM)] * 4 + [vmem],
        out_specs=[vmem] * 4,
        out_shape=[jax.ShapeDtypeStruct((rows, feats), bf16)] * 4,
        scratch_shapes=[
            pltpu.VMEM((rows, feats), bf16),
            pltpu.VMEM((rows, feats), bf16),
            pltpu.VMEM((rows, feats), bf16),
            pltpu.VMEM((rows, feats), bf16),
            pltpu.VMEM((rows, feats), f32),
            pltpu.VMEM((rows, feats), f32),
            pltpu.VMEM((2, TAIL, feats), bf16),
            pltpu.VMEM((2 * half, HEAD_DIM), f32),
            pltpu.VMEM((TAIL, 2 * TAIL + slots), f32),
            pltpu.VMEM((rows - TAIL, rows - OFF + slots), f32),
            pltpu.VMEM((2, TAIL, feats), bf16),
            pltpu.VMEM((2, TAIL, feats), bf16),
            pltpu.VMEM((shards, 2 * half, HEAD_DIM), bf16),
            pltpu.VMEM((shards, 2 * half, HEAD_DIM), bf16),
            pltpu.VMEM((shards, 2 * half, HEAD_DIM), bf16),
            pltpu.VMEM((shards * half, HEAD_DIM), f32),
            pltpu.VMEM((shards * half, HEAD_DIM), f32),
            pltpu.VMEM((shards * half, HEAD_DIM), f32),
            pltpu.VMEM((shards * half, HEAD_DIM), f32),
            pltpu.SemaphoreType.DMA((2, steps)),
            pltpu.SemaphoreType.DMA((2, steps)),
            pltpu.SemaphoreType.DMA((shards,)),
            pltpu.SemaphoreType.DMA((shards,)),
            pltpu.SemaphoreType.DMA((steps,)),
            pltpu.SemaphoreType.DMA((steps,)),
            pltpu.SemaphoreType.DMA((shards,)),
            pltpu.SemaphoreType.DMA((shards,)),
            pltpu.SemaphoreType.DMA((4,)),
        ],
        compiler_params=pltpu.CompilerParams(
            vmem_limit_bytes=51700 * 1024, collective_id=0, has_side_effects=True
        ),
        cost_estimate=pl.CostEstimate(
            flops=10 * rows * columns * feats,
            bytes_accessed=24 * rows * feats,
            transcendentals=HEADS * rows * columns,
        ),
    )(query_rows, key_rows, value_rows, out_grad, own_slots)


def body(query_rows, key_rows, value_rows, out_grad):
    rows, feats = query_rows.shape
    shard = lax.axis_index("seq")
    lead = (shard * rows + OFF) % BLOCK
    index = [BLOCK - 1 - lead + BLOCK * i for i in range(SLOT_DEV)]
    own_slots = jnp.stack([
        jnp.concatenate([
            jnp.where(i < rows, lax.dynamic_slice_in_dim(array, jnp.minimum(i, rows - 1), 1, 0), 0)
            for i in index
        ])
        for array in (key_rows, value_rows)
    ])
    return tuple(
        attention(query_rows, key_rows, value_rows, out_grad, own_slots.reshape(-1, HEAD_DIM))
    )


def solution(mesh):
    spec = P(("groups", "seq"), None)
    return jax.shard_map(
        body, mesh=mesh, in_specs=(spec,) * 4, out_specs=(spec,) * 4, check_vma=False
    )
```
